256 devices in a mesh: ab: 16 (over z_hi, x), ij: 16 (over z_lo, y, core).
Axes of the slice: x: 4, y: 4, z: 8 (z_hi: 4, z_lo: 2; z = z_hi * 2 + z_lo), core: 2. Of those that a mesh axis runs over, the one named last changes fastest.
Arguments:
- partners: int32 [16, 9], P('ab'), may hold values from -1 to 15, as said below
- cholesky: float32 [1536, 16, 4096], P('ab', None, 'ij'), may hold values from -0.3 to 0.3
- amplitudes: float32 [16, 64], P('ij'), may hold values from -6 to 6
Outputs:
- residual: float32 [144, 16, 9216], P('ab', 'ij')
The draws below stay inside these ranges and needn't reach their ends.
Inputs may be any that keep to these rules, and one draw needn't show every extreme that they name: partners[d, 0] = d; every unordered pair of blocks, equal ones included, stands exactly once in the whole table; the blocks in one row are distinct; -1 marks an empty slot, at most one per row and only in the last slot.
All inputs are finite; a program needn't handle non-finite values.
Results may differ from the reference program's by a relative error of at most 0.0003.
Values sent between devices are 32-bit elements; how exact they have to be, the bound alone decides.
A program may use at most 128 MiB of HBM per device.

```python
import jax
import jax.numpy as jnp
from jax import lax

VB = 96
CB = 8
Q = 4096
V = 1536
IJ = 16
PD = 9
N_AB = 16


def draw_partners(key, part):
    key = jax.random.fold_in(key, 11)
    places = jax.random.permutation(key, N_AB).astype(jnp.int32)
    owners = jnp.argsort(places).astype(jnp.int32)
    half_count = N_AB // 2
    offsets = jnp.arange(half_count, dtype=jnp.int32)
    partner = owners[(places[:, None] + offsets[None, :]) % N_AB]
    final_slot = jnp.where(places < half_count, owners[(places + half_count) % N_AB], -1)
    return jnp.concatenate([partner, final_slot[:, None]], axis=1).astype(jnp.int32)


def level_of(key, shape, split, low, largest):
    def one(dim, shards_of):
        draws = jax.random.uniform(jax.random.fold_in(jax.random.fold_in(key, 6), dim), (shards_of,), jnp.float32, low / len(split), largest / len(split))
        return jnp.repeat(jnp.exp(draws), shape[dim] // shards_of).reshape((-1,) + (1,) * (len(shape) - dim - 1))

    gain = one(*split[0])
    for cut in split[1:]:
        gain = gain * one(*cut)
    return gain


def scatter_about(own_key, shape, scale, most, pieces=(), kind=jnp.bfloat16):
    factor_of = level_of(own_key, shape, pieces, -0.22, 0.18) if pieces else 1.0
    values = jax.random.normal(own_key, shape, jnp.float32) * scale * factor_of
    return jnp.minimum(jnp.maximum(values, -most), most).astype(kind)


def setup_inputs(seed: int = 0) -> dict:
    seeds = jax.random.split(jax.random.key(seed), 4)
    partners = draw_partners(jax.random.fold_in(seeds[3], 71), 0)
    cholesky = scatter_about(seeds[1], (V, 2 * CB, Q), 0.05, 0.3, ((0, 16), (2, 16)), jnp.float32)
    amplitudes = scatter_about(seeds[2], (IJ, CB * CB), 1.0, 6.0, ((0, 16),), jnp.float32)
    return dict(partners=partners, cholesky=cholesky, amplitudes=amplitudes)


def contract(upper, lower, amps):
    width = upper.shape[0]
    window = upper.shape[1]
    left = upper.reshape(width * window, -1)
    right = lower.reshape(width * window, -1)
    tiles = lax.dot_general(left, right, (((1,), (1,)), ((), ())), precision=lax.Precision.HIGHEST, preferred_element_type=jnp.float32)
    tiles = tiles.reshape(width, window, width, window)
    result = jnp.einsum("acbd,icd->iab", tiles, amps, precision=lax.Precision.HIGHEST)
    return result.reshape(amps.shape[0], width * width)


def reference(partners, cholesky, amplitudes):
    amps = amplitudes.reshape(IJ, CB, CB)
    flat_partners = partners.reshape(-1).astype(jnp.int32)
    flat_owners = (jnp.arange(N_AB * PD, dtype=jnp.int32) // PD).astype(jnp.int32)

    def tile_for(pair):
        owner, partner = pair
        valid = (partner >= 0).astype(jnp.float32)
        other = jnp.maximum(partner, 0)
        upper_block = jnp.maximum(owner, other).astype(jnp.int32)
        lower_block = jnp.minimum(owner, other).astype(jnp.int32)
        upper = lax.dynamic_slice_in_dim(cholesky, (upper_block * VB).astype(jnp.int32), VB, 0)[:, :CB]
        lower = lax.dynamic_slice_in_dim(cholesky, (lower_block * VB).astype(jnp.int32), VB, 0)[:, CB:]
        return contract(upper, lower, amps) * valid

    return lax.map(tile_for, (flat_owners, flat_partners))
```

```python
import jax
import jax.numpy as jnp
from jax import lax
from jax.experimental import pallas as pl
from jax.experimental.pallas import tpu as pltpu
from jax.sharding import PartitionSpec as P

MESH = pl.DeviceIdType.MESH
F32 = jnp.float32
BF16 = jnp.bfloat16
VB = 96
CB = 8
QL = 256
ROWS = VB * CB
NX = 4
LT = 3
IJ = 16


def split(v):
    hi = v.astype(BF16)
    lo = (v - hi.astype(F32)).astype(BF16)
    return hi, lo


def ladder(
    partners, chol, amp, out,
    gbuf, sbuf, tbuf, left, right, tile, part, cbuf, ybuf, piece, rall,
    lsem, gs, gr, ps, pr, ts, tr, cs, cr, ys, yr, rs, rr,
):
    ab = lax.axis_index("ab")
    ij = lax.axis_index("ij")
    z, x = lax.div(ab, 4), lax.rem(ab, 4)
    zl, y, core = lax.div(ij, 8), lax.rem(lax.div(ij, 2), 4), lax.rem(ij, 2)

    def dev(z_, x_, zl_, y_, core_):
        return (z_ * 4 + x_, zl_ * 8 + y_ * 2 + core_)

    def mod4(v):
        return lax.rem(v + 8, 4)

    def gathered_half(z_):
        return jnp.where(zl == 0, jnp.where(z_ == 3, 0, 1), jnp.where(z_ == 0, 1, 0))

    sgn = 1 - 2 * zl
    gt = gathered_half(z)
    xl, xr, x2 = mod4(x - 1), mod4(x + 1), mod4(x + 2)
    yl, yr_, y2 = mod4(y - 1), mod4(y + 1), mod4(y + 2)
    zd = mod4(z - sgn)
    has2 = jnp.where(zl == 0, z < 2, z >= 2)
    forwards = jnp.logical_and(z >= 1, z <= 2)
    slot = core * 8 + y * 2 + zl

    barrier = pltpu.get_barrier_semaphore()
    peers = [(ab, lax.rem(ij + n, 16)) for n in range(1, 16)]
    for n in range(1, 4):
        for o in range(2):
            peers.append(dev(z, mod4(x + n), o, y, core))
            peers.append(dev(mod4(z + n), x, o, y, core))
    for peer in peers:
        pl.semaphore_signal(barrier, inc=1, device_id=peer, device_id_type=MESH)
    pl.semaphore_wait(barrier, len(peers))

    def remote(src, dst, send, recv, device):
        return pltpu.make_async_remote_copy(
            src_ref=src, dst_ref=dst, send_sem=send, recv_sem=recv, device_id=device, device_id_type=MESH
        )

    own_g = chol.at[:, gt]
    g_right = remote(own_g, gbuf.at[x], gs.at[0], gr.at[0], dev(z, xr, zl, y, core))
    g_left = remote(own_g, gbuf.at[x], gs.at[1], gr.at[1], dev(z, xl, zl, y, core))
    p_send = remote(
        chol.at[:, 1 - gathered_half(zd)], sbuf.at[1], ps.at[0], pr.at[0], dev(zd, x, zl, y, core)
    )
    g_right.start()
    g_left.start()
    p_send.start()
    local_g = pltpu.make_async_copy(own_g, gbuf.at[x], lsem.at[0])
    local_s = pltpu.make_async_copy(chol.at[:, 1 - gt], sbuf.at[0], lsem.at[1])
    local_g.start()
    local_s.start()
    t_sends = [
        remote(amp, tbuf.at[slot], ts.at[n - 1], tr.at[slot], (ab, lax.rem(ij + n, 16)))
        for n in range(1, 16)
    ]
    for c in t_sends:
        c.start()
    tbuf[slot] = amp[...]

    gview = gbuf.reshape(NX, VB * 2 * CB, 128)
    sview = sbuf.reshape(3, VB * 2 * CB, 128)

    def load_half(view, n, c):
        return jnp.concatenate(
            [view[n, pl.ds(h * CB + c, VB, stride=2 * CB), :] for h in range(2)], axis=1
        )

    def convert_g(n):
        base = pl.multiple_of(n * VB, 32)
        for e in range(CB):
            hi, lo = split(load_half(gview, n, e))
            right[e, pl.ds(base, VB), 0:QL] = hi
            right[e, pl.ds(base, VB), QL:2 * QL] = lo
            right[e, pl.ds(base, VB), 2 * QL:3 * QL] = hi

    def convert_s(k):
        for c in range(CB):
            hi, lo = split(load_half(sview, k, c))
            left[c * VB:(c + 1) * VB, 0:QL] = hi
            left[c * VB:(c + 1) * VB, QL:2 * QL] = hi
            left[c * VB:(c + 1) * VB, 2 * QL:3 * QL] = lo

    local_g.wait()
    local_s.wait()
    convert_g(x)
    convert_s(0)

    for n in range(1, 16):
        peer = lax.rem(ij + n, 16)
        other = lax.rem(peer, 2) * 8 + lax.rem(lax.div(peer, 2), 4) * 2 + lax.div(peer, 8)
        remote(amp, tbuf.at[other], ts.at[0], tr.at[other], (ab, peer)).wait_recv()
    tv = jnp.where(gt == 1, tbuf[:, 1, :], tbuf[:, 0, :])
    thi, tlo = split(tv)
    lane = lax.broadcasted_iota(jnp.int32, (IJ, 128), 1)
    tlo = jnp.where(lane < 64, tlo.astype(F32), 0.0).astype(BF16)
    tm = jnp.concatenate([thi, tlo], axis=0)

    remote(own_g, gbuf.at[xl], gs.at[0], gr.at[0], dev(z, xl, zl, y, core)).wait_recv()
    f_right = remote(
        gbuf.at[xl, pl.ds(0, 48)], gbuf.at[xl, pl.ds(0, 48)], gs.at[2], gr.at[2], dev(z, xr, zl, y, core)
    )
    f_right.start()
    remote(own_g, gbuf.at[xr], gs.at[1], gr.at[1], dev(z, xr, zl, y, core)).wait_recv()
    f_left = remote(
        gbuf.at[xr, pl.ds(48, 48)], gbuf.at[xr, pl.ds(48, 48)], gs.at[3], gr.at[3], dev(z, xl, zl, y, core)
    )
    f_left.start()
    p_send.wait_recv()
    p_forward = remote(sbuf.at[1], sbuf.at[2], ps.at[1], pr.at[1], dev(zd, x, zl, y, core))

    @pl.when(forwards)
    def _():
        p_forward.start()

    convert_g(xl)
    convert_g(xr)
    remote(
        gbuf.at[x2, pl.ds(0, 48)], gbuf.at[x2, pl.ds(0, 48)], gs.at[2], gr.at[2], dev(z, xl, zl, y, core)
    ).wait_recv()
    remote(
        gbuf.at[x2, pl.ds(48, 48)], gbuf.at[x2, pl.ds(48, 48)], gs.at[3], gr.at[3], dev(z, xr, zl, y, core)
    ).wait_recv()
    convert_g(x2)

    def stage1():
        def column(e, carry):
            for m in range(3):
                t = lax.dot_general(
                    left[m * 256:(m + 1) * 256, :], right[e],
                    (((1,), (1,)), ((), ())), preferred_element_type=F32,
                )
                for l in range(LT):
                    tile[e * LT + l, m * 256:(m + 1) * 256, :] = t[:, l * 128:(l + 1) * 128]
            return carry

        lax.fori_loop(0, CB, column, 0)

    def stage2(k):
        def row(n, carry):
            rhs = []
            for u in range(2):
                a = n * 2 + u
                s = jnp.concatenate(
                    [
                        jnp.concatenate(
                            [tile[e * LT + l, pl.ds(a, CB, stride=VB), :] for l in range(LT)], axis=1
                        )
                        for e in range(CB)
                    ],
                    axis=0,
                )
                hi, lo = split(s)
                rhs.append(jnp.concatenate([hi, lo], axis=0))
            r = lax.dot_general(
                tm, jnp.concatenate(rhs, axis=1), (((1,), (0,)), ((), ())), preferred_element_type=F32
            )
            r = r[:IJ] + r[IJ:]
            for u in range(2):
                for l in range(LT):
                    part[k, l, pl.ds(n * 2 + u, IJ, stride=VB), :] = r[
                        :, (u * LT + l) * 128:(u * LT + l + 1) * 128
                    ]
            return carry

        lax.fori_loop(0, VB // 2, row, 0)

    base = pl.multiple_of(core * 768, 768)
    away = pl.multiple_of((1 - core) * 768, 768)
    sibling = dev(z, x, zl, y, 1 - core)
    y_left, y_right = dev(z, x, zl, yl, core), dev(z, x, zl, yr_, core)

    def part_rows(k, y_, o):
        return part.at[k, :, pl.ds(pl.multiple_of(base + y_ * 192 + o * 96, 32), 96), :]

    def core_copy(k):
        return remote(part.at[k, :, pl.ds(away, 768), :], cbuf.at[k], cs.at[k], cr.at[k], sibling)

    def y_copies(k):
        return [
            remote(part_rows(k, y2, 0), ybuf.at[k, 0], ys.at[k, 0], yr.at[k, 0], y_right),
            remote(part_rows(k, yr_, 1), ybuf.at[k, 1], ys.at[k, 1], yr.at[k, 1], y_right),
            remote(part_rows(k, y2, 1), ybuf.at[k, 2], ys.at[k, 2], yr.at[k, 2], y_left),
            remote(part_rows(k, yl, 0), ybuf.at[k, 3], ys.at[k, 3], yr.at[k, 3], y_left),
            remote(part_rows(k, yr_, 0), ybuf.at[k, 4], ys.at[k, 4], yr.at[k, 4], y_right),
            remote(part_rows(k, yl, 1), ybuf.at[k, 5], ys.at[k, 5], yr.at[k, 5], y_left),
        ]

    def y_step1(k):
        core_copy(k).wait_recv()

        def add(n, carry):
            for l in range(LT):
                at = pl.ds(pl.multiple_of(base + n * VB, 32), VB)
                part[k, l, at, :] = part[k, l, at, :] + cbuf[k, l, pl.ds(pl.multiple_of(n * VB, 32), VB), :]
            return carry

        lax.fori_loop(0, 8, add, 0)
        for c in y_copies(k)[:4]:
            c.start()

    def merge(k, y_, o, n):
        at = pl.ds(pl.multiple_of(base + y_ * 192 + o * 96, 32), VB)
        for l in range(LT):
            part[k, l, at, :] = part[k, l, at, :] + ybuf[k, n, l]

    def y_step2(k):
        copies = y_copies(k)
        copies[0].wait_recv()
        merge(k, yr_, 0, 0)
        copies[4].start()
        copies[2].wait_recv()
        merge(k, yl, 1, 2)
        copies[5].start()

    def routes(k, op):
        zk = mod4(z + sgn * k)
        for xp in range(NX):
            valid = jnp.where(gt == 1, xp <= x, xp >= x)
            for o in range(2):
                src = piece.at[k, xp, o]

                def go(slot_, remote_ok, local_ok, device, n):
                    @pl.when(remote_ok)
                    def _():
                        c = remote(src, rall.at[zl, slot_], rs.at[k, xp, o, n], rr.at[zl, slot_], device)
                        if op == "start":
                            c.start()
                        else:
                            c.wait_send()

                    if op == "start":
                        @pl.when(local_ok)
                        def _():
                            pltpu.make_async_copy(src, rall.at[zl, slot_], rr.at[zl, slot_]).start()

                here = jnp.logical_and(xp == x, zl == o)
                if k == 0:
                    no = jnp.bool_(False)
                    go(zk * 4 + x, jnp.logical_and(valid, xp != x), no, dev(z, xp, o, y, core), 0)
                    go(
                        z * 4 + xp,
                        jnp.logical_and(valid, zl != o),
                        jnp.logical_and(valid, zl == o),
                        dev(z, x, o, y, core),
                        1,
                    )
                else:
                    go(zk * 4 + x, jnp.logical_not(here), here, dev(z, xp, o, y, core), 0)
                    go(z * 4 + xp, jnp.bool_(True), jnp.bool_(False), dev(zk, x, o, y, core), 1)

    def final(k):
        copies = y_copies(k)
        pairs = ((3, 4), (1, 5))
        for o in range(2):
            copies[pairs[o][0]].wait_recv()
            copies[pairs[o][1]].wait_recv()
            at = pl.ds(pl.multiple_of(base + y * 192 + o * 96, 32), VB)
            v = jnp.concatenate(
                [part[k, l, at, :] + ybuf[k, pairs[o][0], l] + ybuf[k, pairs[o][1], l] for l in range(LT)], axis=1
            )
            blank = jnp.zeros((VB, 128 - VB), F32)
            for xp in range(NX):
                w = v[:, xp * VB:(xp + 1) * VB]
                square = jnp.concatenate([w, blank], axis=1)
                square = jnp.concatenate([square, jnp.zeros((128 - VB, 128), F32)], axis=0)

                @pl.when(gt == 1)
                def _():
                    piece[k, xp, o] = square[:VB]

                @pl.when(gt == 0)
                def _():
                    piece[k, xp, o] = square.T[:VB]

        routes(k, "start")

    stage1()
    stage2(0)
    core_copy(0).start()
    convert_s(1)
    stage1()
    y_step1(0)
    stage2(1)
    core_copy(1).start()
    y_step2(0)

    @pl.when(has2)
    def _():
        p_forward.wait_recv()
        convert_s(2)
        stage1()

    y_step1(1)
    final(0)

    @pl.when(has2)
    def _():
        stage2(2)
        core_copy(2).start()

    y_step2(1)

    @pl.when(has2)
    def _():
        y_step1(2)

    final(1)

    @pl.when(has2)
    def _():
        y_step2(2)
        final(2)

    for s in range(2):
        for p in range(16):
            pltpu.make_async_copy(rall.at[s, p], rall.at[s, p], rr.at[s, p]).wait()
    for s in range(out.shape[0]):
        p = partners[0, s]
        at = jnp.maximum(p, 0)
        out[s] = jnp.where(p >= 0, rall[0, at] + rall[1, at], 0.0)

    for c in [g_right, g_left, p_send, f_right, f_left] + t_sends:
        c.wait_send()

    @pl.when(forwards)
    def _():
        p_forward.wait_send()

    def drain(k):
        core_copy(k).wait_send()
        for c in y_copies(k):
            c.wait_send()
        routes(k, "wait")

    drain(0)
    drain(1)

    @pl.when(has2)
    def _():
        drain(2)


def local(partners, cholesky, amplitudes):
    slots = partners.shape[1]
    chol = cholesky.reshape(VB, 2, CB, 2, 128).transpose(0, 1, 3, 2, 4)
    flat = amplitudes.reshape(1, CB * CB)
    turned = amplitudes.reshape(CB, CB).T.reshape(1, CB * CB)
    amp = jnp.concatenate(
        [jnp.tile(flat, (1, 2)), jnp.tile(turned, (1, 2)), jnp.zeros((6, 128), F32)], axis=0
    )
    dma = pltpu.SemaphoreType.DMA
    res = pl.pallas_call(
        ladder,
        out_shape=jax.ShapeDtypeStruct((slots, VB, 128), F32),
        in_specs=[
            pl.BlockSpec(memory_space=pltpu.SMEM),
            pl.BlockSpec(memory_space=pl.ANY),
            pl.BlockSpec(memory_space=pltpu.VMEM),
        ],
        out_specs=pl.BlockSpec(memory_space=pltpu.VMEM),
        scratch_shapes=[
            pltpu.VMEM((NX, VB, 2, CB, 128), F32),
            pltpu.VMEM((3, VB, 2, CB, 128), F32),
            pltpu.VMEM((IJ, 8, 128), F32),
            pltpu.VMEM((ROWS, 3 * QL), BF16),
            pltpu.VMEM((CB, NX * VB, 3 * QL), BF16),
            pltpu.VMEM((CB * LT, ROWS, 128), F32),
            pltpu.VMEM((3, LT, IJ * VB, 128), F32),
            pltpu.VMEM((3, LT, 8 * VB, 128), F32),
            pltpu.VMEM((3, 6, LT, VB, 128), F32),
            pltpu.VMEM((3, NX, 2, VB, 128), F32),
            pltpu.VMEM((2, 16, VB, 128), F32),
            dma((2,)),
            dma((4,)), dma((4,)),
            dma((2,)), dma((2,)),
            dma((15,)), dma((16,)),
            dma((3,)), dma((3,)),
            dma((3, 6)), dma((3, 6)),
            dma((3, NX, 2, 2)), dma((2, 16)),
        ],
        compiler_params=pltpu.CompilerParams(
            collective_id=0, has_side_effects=True, vmem_limit_bytes=56 * 1024 * 1024
        ),
    )(partners, chol, amp)
    return res[:, :, :VB].reshape(slots, 1, VB * VB)


def solution(mesh):
    return jax.shard_map(
        local,
        mesh=mesh,
        in_specs=(P("ab", None), P("ab", None, "ij"), P("ij", None)),
        out_specs=P("ab", "ij", None),
        check_vma=False,
    )
```

```python
import jax
import jax.numpy as jnp
from jax import lax
from jax.experimental import pallas as pl
from jax.experimental.pallas import tpu as pltpu
from jax.sharding import PartitionSpec as P

MESH = pl.DeviceIdType.MESH
F32 = jnp.float32
BF16 = jnp.bfloat16
VB = 96
CB = 8
QL = 256
ROWS = VB * CB
NX = 4
LT = 3
CH = 32
IJ = 16


def split(v):
    hi = v.astype(BF16)
    lo = (v - hi.astype(F32)).astype(BF16)
    return hi, lo


def ladder(
    partners, chol, amp, out,
    gbuf, sbuf, abuf, tbuf, wide, left, right, tile, part, cbuf, ybuf, square, piece, rall,
    lsem, gs, gr, ps, pr, ts, tr, cs, cr, ys, yr, rs, rr,
):
    ab = lax.axis_index("ab")
    ij = lax.axis_index("ij")
    z, x = lax.div(ab, 4), lax.rem(ab, 4)
    zl, y, core = lax.div(ij, 8), lax.rem(lax.div(ij, 2), 4), lax.rem(ij, 2)

    def dev(z_, x_, zl_, y_, core_):
        return (z_ * 4 + x_, zl_ * 8 + y_ * 2 + core_)

    def mod4(v):
        return lax.rem(v + 8, 4)

    def gathered_half(z_):
        return jnp.where(zl == 0, jnp.where(z_ == 3, 0, 1), jnp.where(z_ == 0, 1, 0))

    sgn = 1 - 2 * zl
    gt = gathered_half(z)
    xl, xr, x2 = mod4(x - 1), mod4(x + 1), mod4(x + 2)
    yl, yr_, y2 = mod4(y - 1), mod4(y + 1), mod4(y + 2)
    zd = mod4(z - sgn)
    has2 = jnp.where(zl == 0, z < 2, z >= 2)
    forwards = jnp.logical_and(z >= 1, z <= 2)
    slot = core * 8 + y * 2 + zl

    barrier = pltpu.get_barrier_semaphore()
    peers = [(ab, lax.rem(ij + n, 16)) for n in range(1, 16)]
    for n in range(1, 4):
        for o in range(2):
            peers.append(dev(z, mod4(x + n), o, y, core))
            peers.append(dev(mod4(z + n), x, o, y, core))
    for peer in peers:
        pl.semaphore_signal(barrier, inc=1, device_id=peer, device_id_type=MESH)
    own_g = chol.at[:, gt]
    local_g = pltpu.make_async_copy(own_g, gbuf.at[x], lsem.at[0])
    local_s = pltpu.make_async_copy(chol.at[:, 1 - gt], sbuf.at[0], lsem.at[1])
    local_g.start()
    local_s.start()
    row = jnp.concatenate([amp[...], jnp.zeros((1, 64), F32)], axis=1)
    abuf[...] = jnp.broadcast_to(row, (8, 128))
    pl.semaphore_wait(barrier, len(peers))

    def remote(src, dst, send, recv, device):
        return pltpu.make_async_remote_copy(
            src_ref=src, dst_ref=dst, send_sem=send, recv_sem=recv, device_id=device, device_id_type=MESH
        )

    to_right, to_left = dev(z, xr, zl, y, core), dev(z, xl, zl, y, core)
    to_down = dev(zd, x, zl, y, core)

    def g_chunk(j, d):
        return remote(
            chol.at[pl.ds(j * CH, CH), gt], gbuf.at[x, pl.ds(j * CH, CH)], gs.at[j, d], gr.at[j, d],
            (to_right, to_left)[d],
        )

    def g_from(j, d):
        at = gbuf.at[(xl, xr)[d], pl.ds(j * CH, CH)]
        return remote(at, at, gs.at[j, d], gr.at[j, d], (to_right, to_left)[d])

    def g_forward(j, d):
        at = gbuf.at[(xl, xr)[d], pl.ds(j * CH + d * 16, 16)]
        return remote(at, at, gs.at[j, 2 + d], gr.at[j, 2 + d], (to_right, to_left)[d])

    def g_behind(j, d):
        at = gbuf.at[x2, pl.ds(j * CH + d * 16, 16)]
        return remote(at, at, gs.at[j, 2 + d], gr.at[j, 2 + d], (to_right, to_left)[d])

    def p_chunk(m):
        return remote(
            chol.at[pl.ds(m * CH, CH), 1 - gathered_half(zd)], sbuf.at[1, pl.ds(m * CH, CH)],
            ps.at[0, m], pr.at[0, m], to_down,
        )

    def p_forward(m):
        return remote(
            sbuf.at[1, pl.ds(m * CH, CH)], sbuf.at[2, pl.ds(m * CH, CH)], ps.at[1, m], pr.at[1, m], to_down
        )

    for d in range(2):
        g_chunk(0, d).start()
    for m in range(3):
        p_chunk(m).start()
    t_sends = [
        remote(abuf, tbuf.at[slot], ts.at[n - 1], tr.at[slot], (ab, lax.rem(ij + n, 16)))
        for n in range(1, 16)
    ]
    for c in t_sends:
        c.start()
    tbuf[slot] = abuf[...]

    gview = gbuf.reshape(NX, VB * 2 * CB, 128)

    def convert_g(n, j):
        for e in range(CB):
            v = jnp.concatenate(
                [gview[n, pl.ds(j * CH * 16 + h * CB + e, CH, stride=2 * CB), :] for h in range(2)], axis=1
            )
            hi, lo = split(v)
            at = pl.ds(pl.multiple_of(e * 128 + n * CH, CH), CH)
            right[j, at, 0:QL] = hi
            right[j, at, QL:2 * QL] = lo
            right[j, at, 2 * QL:3 * QL] = hi

    def convert_s(k, m):
        for h in range(2):
            v = sbuf[k, pl.ds(m * CH, CH), h].reshape(CH * CB, 128)
            hi, lo = split(v)
            at = pl.ds(m * CH * CB, CH * CB)
            left[k, at, h * 128:h * 128 + 128] = hi
            left[k, at, QL + h * 128:QL + h * 128 + 128] = hi
            left[k, at, 2 * QL + h * 128:2 * QL + h * 128 + 128] = lo

    local_g.wait()
    local_s.wait()
    for j in range(LT):
        convert_g(x, j)
        convert_s(0, j)

    for n in range(1, 16):
        peer = lax.rem(ij + n, 16)
        other = lax.rem(peer, 2) * 8 + lax.rem(lax.div(peer, 2), 4) * 2 + lax.div(peer, 8)
        remote(abuf, tbuf.at[other], ts.at[0], tr.at[other], (ab, peer)).wait_recv()
    source = lax.broadcasted_iota(jnp.int32, (128, 512), 0)
    target = lax.rem(lax.broadcasted_iota(jnp.int32, (128, 512), 1), 64)
    turned = lax.rem(target, 8) * 8 + lax.div(target, 8)
    pick = jnp.where(source == jnp.where(gt == 1, turned, target), 1.0, 0.0).astype(BF16)
    same = lax.rem(lax.broadcasted_iota(jnp.int32, (128, 512), 0), 8) == lax.div(
        lax.broadcasted_iota(jnp.int32, (128, 512), 1), 64
    )
    for n, v in enumerate(split(tbuf[:, 0, :])):
        w = jnp.dot(v, pick, preferred_element_type=F32)
        w = jnp.broadcast_to(w[:, None, :], (IJ, 8, 512)).reshape(128, 512)
        wide[n * 128:(n + 1) * 128] = jnp.where(same, w, 0.0).astype(BF16)

    def stage1(k, j, m):
        def column(e2, carry):
            at = pl.ds(pl.multiple_of(e2 * 256, 256), 256)
            for n in range(3):
                t = lax.dot_general(
                    left[k, (n if m is None else m) * 256:((n if m is None else m) + 1) * 256, :],
                    right[n if j is None else j, at, :],
                    (((1,), (1,)), ((), ())), preferred_element_type=F32,
                )
                for u in range(2):
                    tile[e2 * 2 + u, n * 256:(n + 1) * 256, :] = t[:, u * 128:(u + 1) * 128]
            return carry

        lax.fori_loop(0, CB // 2, column, 0)

    def stage2(k, j, m):
        def rows(n, carry):
            his, los = [], []
            for u in range(2):
                base_ = (n * 2 + u) * 64
                s = jnp.concatenate(
                    [tile[e, pl.ds(pl.multiple_of(base_ + a * 8, 8), 8), :] for a in range(8) for e in range(CB)],
                    axis=0,
                )
                hi, lo = split(s)
                his.append(hi)
                los.append(lo)
            r = jnp.dot(wide[...], jnp.concatenate(his, axis=1), preferred_element_type=F32)
            q = jnp.dot(wide[0:128], jnp.concatenate(los, axis=1), preferred_element_type=F32)
            r = r[:128] + r[128:] + q
            for u in range(2):
                v = r[:, u * 128:(u + 1) * 128].reshape(IJ, 8, 128)
                item = n * 2 + u
                if m is None:
                    part[k, j, :, pl.ds(pl.multiple_of(item * 8, 8), 8), :] = v
                else:
                    at = pl.multiple_of(m * CH + lax.rem(item, 4) * 8, 8)
                    part[k, lax.div(item, 4), :, pl.ds(at, 8), :] = v
            return carry

        lax.fori_loop(0, 6, rows, 0)

    units = [(0, 0, None), (0, 1, None), (1, 0, None), (1, 1, None), (0, 2, None), (1, 2, None)]
    units += [(2, None, m) for m in range(3)]
    base, away = core * 8, (1 - core) * 8
    sibling = dev(z, x, zl, y, 1 - core)
    y_left, y_right = dev(z, x, zl, yl, core), dev(z, x, zl, yr_, core)

    def spans(n):
        k, j, m = units[n]
        if m is None:
            return k, pl.ds(j, 1), pl.ds(0, VB)
        return k, pl.ds(0, LT), pl.ds(m * CH, CH)

    def core_copy(n):
        k, l, a = spans(n)
        return remote(
            part.at[k, l, pl.ds(away, 8), a], cbuf.at[k, l, pl.ds(0, 8), a], cs.at[n], cr.at[n], sibling
        )

    def y_copies(n):
        k, l, a = spans(n)

        def one(c, y_, o, device):
            return remote(
                part.at[k, l, base + y_ * 2 + o, a], ybuf.at[k, c, l, a], ys.at[n, c], yr.at[n, c], device
            )

        return [
            one(0, y2, 0, y_right), one(1, yr_, 1, y_right), one(2, y2, 1, y_left),
            one(3, yl, 0, y_left), one(4, yr_, 0, y_right), one(5, yl, 1, y_left),
        ]

    def lanes_of(n):
        k, j, m = units[n]
        return k, ([j] if m is None else list(range(LT))), (slice(0, VB) if m is None else slice(m * CH, m * CH + CH))

    def y_step1(n):
        core_copy(n).wait_recv()
        k, ls, a = lanes_of(n)

        def add(i, carry):
            for l in ls:
                part[k, l, base + i, a, :] = part[k, l, base + i, a, :] + cbuf[k, l, i, a, :]
            return carry

        lax.fori_loop(0, 8, add, 0)
        for c in y_copies(n)[:4]:
            c.start()

    def y_step2(n):
        copies = y_copies(n)
        k, ls, a = lanes_of(n)
        for first, i, then in ((0, base + yr_ * 2, 4), (2, base + yl * 2 + 1, 5)):
            copies[first].wait_recv()
            for l in ls:
                part[k, l, i, a, :] = part[k, l, i, a, :] + ybuf[k, first, l, a, :]
            copies[then].start()

    def routes(k, op):
        zk = mod4(z + sgn * k)
        for xp in range(NX):
            valid = jnp.where(gt == 1, xp <= x, xp >= x)
            for o in range(2):
                src = piece.at[k, xp, o]

                def go(slot_, remote_ok, local_ok, device, n):
                    @pl.when(remote_ok)
                    def _():
                        c = remote(src, rall.at[zl, slot_], rs.at[k, xp, o, n], rr.at[zl, slot_], device)
                        if op == "start":
                            c.start()
                        else:
                            c.wait_send()

                    if op == "start":
                        @pl.when(local_ok)
                        def _():
                            pltpu.make_async_copy(src, rall.at[zl, slot_], rr.at[zl, slot_]).start()

                here = jnp.logical_and(xp == x, zl == o)
                if k == 0:
                    no = jnp.bool_(False)
                    go(zk * 4 + x, jnp.logical_and(valid, xp != x), no, dev(z, xp, o, y, core), 0)
                    go(
                        z * 4 + xp,
                        jnp.logical_and(valid, zl != o),
                        jnp.logical_and(valid, zl == o),
                        dev(z, x, o, y, core),
                        1,
                    )
                else:
                    go(zk * 4 + x, jnp.logical_not(here), here, dev(z, xp, o, y, core), 0)
                    go(z * 4 + xp, jnp.bool_(True), jnp.bool_(False), dev(zk, x, o, y, core), 1)

    lane = lax.broadcasted_iota(jnp.int32, (24, 128), 1)
    tall = lax.broadcasted_iota(jnp.int32, (VB, 128), 1)

    def final(k):
        pairs = ((3, 4), (1, 5))
        for n in range(len(units)):
            if units[n][0] == k:
                copies = y_copies(n)
                for c in (1, 3, 4, 5):
                    copies[c].wait_recv()
        for o in range(2):
            v = [
                part[k, l, base + y * 2 + o] + ybuf[k, pairs[o][0], l] + ybuf[k, pairs[o][1], l]
                for l in range(LT)
            ]
            for xp in range(NX):
                turn = [v[l] if l == xp else pltpu.roll(v[l], (l - xp) % 4 * 32, 1) for l in range(LT)]
                w = jnp.where(tall < 32, turn[0], jnp.where(tall < 64, turn[1], turn[2]))

                @pl.when(gt == 1)
                def _():
                    square[0:VB] = w

                @pl.when(gt == 0)
                def _():
                    square[...] = jnp.concatenate([w, jnp.zeros((128 - VB, 128), F32)], axis=0).T

                r = [square[pl.ds(n, 24, stride=4), :] for n in range(4)]
                p = piece.at[k, xp, o]
                p[pl.ds(0, 24, stride=3), :] = jnp.where(lane < 96, r[0], pltpu.roll(r[1], 96, 1))
                p[pl.ds(1, 24, stride=3), :] = jnp.where(lane < 64, pltpu.roll(r[1], 96, 1), pltpu.roll(r[2], 64, 1))
                p[pl.ds(2, 24, stride=3), :] = jnp.where(lane < 32, pltpu.roll(r[2], 64, 1), pltpu.roll(r[3], 32, 1))

        routes(k, "start")

    def begin(n):
        stage1(*units[n])

    def end(n):
        stage2(*units[n])
        core_copy(n).start()

    def gather(j):
        for d in range(2):
            g_from(j, d).wait_recv()
            g_forward(j, d).start()
            if j < 2:
                g_chunk(j + 1, d).start()
        convert_g(xl, j)
        convert_g(xr, j)

    def behind(j):
        for d in range(2):
            g_behind(j, d).wait_recv()
        convert_g(x2, j)

    gather(0)
    behind(0)
    begin(0)
    end(0)
    gather(1)
    behind(1)
    for m in range(3):
        p_chunk(m).wait_recv()

    @pl.when(forwards)
    def _():
        for m in range(3):
            p_forward(m).start()

    begin(1)
    y_step1(0)
    end(1)
    y_step2(0)
    for m in range(3):
        convert_s(1, m)
    begin(2)
    y_step1(1)
    end(2)
    y_step2(1)
    gather(2)
    begin(3)
    y_step1(2)
    end(3)
    y_step2(2)
    behind(2)
    begin(4)
    y_step1(3)
    end(4)
    y_step2(3)
    begin(5)
    y_step1(4)
    end(5)
    y_step2(4)

    @pl.when(has2)
    def _():
        for m in range(3):
            p_forward(m).wait_recv()
            convert_s(2, m)
            begin(6 + m)
            y_step1(5 + m)
            end(6 + m)
            y_step2(5 + m)
            if m < 2:
                final(m)
        y_step1(8)
        y_step2(8)
        final(2)

    @pl.when(jnp.logical_not(has2))
    def _():
        y_step1(5)
        final(0)
        y_step2(5)
        final(1)

    for s in range(2):
        for p in range(16):
            pltpu.make_async_copy(rall.at[s, p], rall.at[s, p], rr.at[s, p]).wait()
    for s in range(out.shape[0]):
        p = partners[0, s]
        at = jnp.maximum(p, 0)
        out[s] = jnp.where(p >= 0, rall[0, at] + rall[1, at], 0.0)

    for j in range(LT):
        for d in range(2):
            g_chunk(j, d).wait_send()
            g_forward(j, d).wait_send()
        p_chunk(j).wait_send()
    for c in t_sends:
        c.wait_send()

    @pl.when(forwards)
    def _():
        for m in range(3):
            p_forward(m).wait_send()

    def drain(n):
        core_copy(n).wait_send()
        for c in y_copies(n):
            c.wait_send()

    for n in range(6):
        drain(n)
    routes(0, "wait")
    routes(1, "wait")

    @pl.when(has2)
    def _():
        for n in range(6, 9):
            drain(n)
        routes(2, "wait")


def local(partners, cholesky, amplitudes):
    slots = partners.shape[1]
    chol = cholesky.reshape(VB, 2, CB, 2, 128).transpose(0, 1, 3, 2, 4)
    dma = pltpu.SemaphoreType.DMA
    res = pl.pallas_call(
        ladder,
        out_shape=jax.ShapeDtypeStruct((slots, 72, 128), F32),
        in_specs=[
            pl.BlockSpec(memory_space=pltpu.SMEM),
            pl.BlockSpec(memory_space=pl.ANY),
            pl.BlockSpec(memory_space=pltpu.VMEM),
        ],
        out_specs=pl.BlockSpec(memory_space=pltpu.VMEM),
        scratch_shapes=[
            pltpu.VMEM((NX, VB, 2, CB, 128), F32),
            pltpu.VMEM((3, VB, 2, CB, 128), F32),
            pltpu.VMEM((8, 128), F32),
            pltpu.VMEM((IJ, 8, 128), F32),
            pltpu.VMEM((256, 512), BF16),
            pltpu.VMEM((3, ROWS, 3 * QL), BF16),
            pltpu.VMEM((LT, CB * 128, 3 * QL), BF16),
            pltpu.VMEM((CB, ROWS, 128), F32),
            pltpu.VMEM((3, LT, IJ, VB, 128), F32),
            pltpu.VMEM((3, LT, 8, VB, 128), F32),
            pltpu.VMEM((3, 6, LT, VB, 128), F32),
            pltpu.VMEM((128, 128), F32),
            pltpu.VMEM((3, NX, 2, 72, 128), F32),
            pltpu.VMEM((2, 16, 72, 128), F32),
            dma((2,)),
            dma((3, 4)), dma((3, 4)),
            dma((2, 3)), dma((2, 3)),
            dma((15,)), dma((16,)),
            dma((9,)), dma((9,)),
            dma((9, 6)), dma((9, 6)),
            dma((3, NX, 2, 2)), dma((2, 16)),
        ],
        compiler_params=pltpu.CompilerParams(
            collective_id=0, has_side_effects=True, vmem_limit_bytes=56 * 1024 * 1024
        ),
    )(partners, chol, amplitudes)
    return res.reshape(slots, 1, VB * VB)


def solution(mesh):
    return jax.shard_map(
        local,
        mesh=mesh,
        in_specs=(P("ab", None), P("ab", None, "ij"), P("ij", None)),
        out_specs=P("ab", "ij", None),
        check_vma=False,
    )
```

```python
import jax
import jax.numpy as jnp
from jax import lax
from jax.experimental import pallas as pl
from jax.experimental.pallas import tpu as pltpu
from jax.sharding import PartitionSpec as P

MESH = pl.DeviceIdType.MESH
F32 = jnp.float32
BF16 = jnp.bfloat16
VB = 96
CB = 8
QL = 256
ROWS = VB * CB
NX = 4
LT = 3
CH = 32
PC = 16
PN = 6
IJ = 16


def split(v):
    hi = v.astype(BF16)
    lo = (v - hi.astype(F32)).astype(BF16)
    return hi, lo


def ladder(
    partners, chol, amp, out,
    gbuf, sbuf, abuf, tbuf, wide, left, leftp, right, tile, part, cbuf, ybuf, zbuf, square, piece, rall,
    lsem, gs, gr, ps, pr, ts, tr, cs, cr, ys, yr, zs, zr, rs, rr,
):
    ab = lax.axis_index("ab")
    ij = lax.axis_index("ij")
    z, x = lax.div(ab, 4), lax.rem(ab, 4)
    zl, y, core = lax.div(ij, 8), lax.rem(lax.div(ij, 2), 4), lax.rem(ij, 2)

    def dev(z_, x_, zl_, y_, core_):
        return (z_ * 4 + x_, zl_ * 8 + y_ * 2 + core_)

    def mod4(v):
        return lax.rem(v + 8, 4)

    gt = jnp.where(z < 2, 1, 0)
    xl, xr, x2 = mod4(x - 1), mod4(x + 1), mod4(x + 2)
    yl, yr_, y2 = mod4(y - 1), mod4(y + 1), mod4(y + 2)
    heavy = lax.rem(z, 2) == 0
    ends = jnp.logical_or(z == 0, z == 3)
    slot = core * 8 + y * 2 + zl

    barrier = pltpu.get_barrier_semaphore()
    peers = [(ab, lax.rem(ij + n, 16)) for n in range(1, 16)]
    for n in range(1, 4):
        peers.append(dev(z, mod4(x + n), zl, y, core))
        peers.append(dev(mod4(z + n), x, zl, y, core))
    for peer in peers:
        pl.semaphore_signal(barrier, inc=1, device_id=peer, device_id_type=MESH)
    own_g = chol.at[:, gt]
    local_g = pltpu.make_async_copy(own_g, gbuf.at[x], lsem.at[0])
    local_s = pltpu.make_async_copy(chol.at[:, 1 - gt], sbuf.at[0], lsem.at[1])
    local_g.start()
    local_s.start()
    row = jnp.concatenate([amp[...], jnp.zeros((1, 64), F32)], axis=1)
    abuf[...] = jnp.broadcast_to(row, (8, 128))
    pl.semaphore_wait(barrier, len(peers))

    def remote(src, dst, send, recv, device):
        return pltpu.make_async_remote_copy(
            src_ref=src, dst_ref=dst, send_sem=send, recv_sem=recv, device_id=device, device_id_type=MESH
        )

    to_right, to_left = dev(z, xr, zl, y, core), dev(z, xl, zl, y, core)

    def g_chunk(j, d):
        return remote(
            chol.at[pl.ds(j * CH, CH), gt], gbuf.at[x, pl.ds(j * CH, CH)], gs.at[j, d], gr.at[j, d],
            (to_right, to_left)[d],
        )

    def g_from(j, d):
        at = gbuf.at[(xl, xr)[d], pl.ds(j * CH, CH)]
        return remote(at, at, gs.at[j, d], gr.at[j, d], (to_right, to_left)[d])

    def g_forward(j, d):
        at = gbuf.at[(xl, xr)[d], pl.ds(j * CH + d * 16, 16)]
        return remote(at, at, gs.at[j, 2 + d], gr.at[j, 2 + d], (to_right, to_left)[d])

    def g_behind(j, d):
        at = gbuf.at[x2, pl.ds(j * CH + d * 16, 16)]
        return remote(at, at, gs.at[j, 2 + d], gr.at[j, 2 + d], (to_right, to_left)[d])

    def p_send(m):
        rows = pl.ds(m * PC, PC)
        to = jnp.where(ends, 2, 1)
        return remote(
            chol.at[rows, 1 - lax.rem(z, 2)], sbuf.at[to, rows], ps.at[0, m], pr.at[to, m],
            dev(3 * (1 - lax.rem(z, 2)), x, zl, y, core),
        )

    def p_send_up(m):
        rows = pl.ds(m * PC, PC)
        return remote(
            chol.at[rows, 1], sbuf.at[1, rows], ps.at[1, m], pr.at[1, m], dev(2, x, zl, y, core)
        )

    def p_relay(m):
        rows = pl.ds(m * PC, PC)
        to = jnp.where(z == 0, 1, 2)
        return remote(
            sbuf.at[2, rows], sbuf.at[to, rows], ps.at[2, m], pr.at[to, m], dev(to, x, zl, y, core)
        )

    def p_wait(k, m):
        at = sbuf.at[k, pl.ds(m * PC, PC)]
        remote(at, at, ps.at[0, m], pr.at[k, m], to_right).wait_recv()

    def relay(m):
        @pl.when(ends)
        def _():
            p_wait(2, m)
            p_relay(m).start()

    for d in range(2):
        g_chunk(0, d).start()
    for m in range(PN):
        p_send(m).start()

    @pl.when(z == 1)
    def _():
        for m in range(PN):
            p_send_up(m).start()

    t_sends = [
        remote(abuf, tbuf.at[slot], ts.at[n - 1], tr.at[slot], (ab, lax.rem(ij + n, 16)))
        for n in range(1, 16)
    ]
    for c in t_sends:
        c.start()
    tbuf[slot] = abuf[...]

    gview = gbuf.reshape(NX, VB * 2 * CB, 128)

    def convert_g(n, j):
        for e in range(CB):
            v = jnp.concatenate(
                [gview[n, pl.ds(j * CH * 16 + h * CB + e, CH, stride=2 * CB), :] for h in range(2)], axis=1
            )
            hi, lo = split(v)
            at = pl.ds(pl.multiple_of(e * 128 + n * CH, CH), CH)
            right[j, at, 0:QL] = hi
            right[j, at, QL:2 * QL] = lo
            right[j, at, 2 * QL:3 * QL] = hi

    def convert_s(k, m):
        for h in range(2):
            v = sbuf[k, pl.ds(m * PC, PC), h].reshape(PC * CB, 128)
            hi, lo = split(v)
            to = left.at[pl.ds(m * PC * CB, PC * CB)] if k == 0 else leftp.at[m, pl.ds((k - 1) * PC * CB, PC * CB)]
            to[:, h * 128:h * 128 + 128] = hi
            to[:, QL + h * 128:QL + h * 128 + 128] = hi
            to[:, 2 * QL + h * 128:2 * QL + h * 128 + 128] = lo

    local_g.wait()
    local_s.wait()
    for j in range(LT):
        convert_g(x, j)
    for m in range(PN):
        convert_s(0, m)

    for n in range(1, 16):
        peer = lax.rem(ij + n, 16)
        other = lax.rem(peer, 2) * 8 + lax.rem(lax.div(peer, 2), 4) * 2 + lax.div(peer, 8)
        remote(abuf, tbuf.at[other], ts.at[0], tr.at[other], (ab, peer)).wait_recv()
    source = lax.broadcasted_iota(jnp.int32, (128, 512), 0)
    target = lax.rem(lax.broadcasted_iota(jnp.int32, (128, 512), 1), 64)
    turned = lax.rem(target, 8) * 8 + lax.div(target, 8)
    pick = jnp.where(source == jnp.where(gt == 1, turned, target), 1.0, 0.0).astype(BF16)
    same = lax.rem(lax.broadcasted_iota(jnp.int32, (128, 512), 0), 8) == lax.div(
        lax.broadcasted_iota(jnp.int32, (128, 512), 1), 64
    )
    for n, v in enumerate(split(tbuf[:, 0, :])):
        w = jnp.dot(v, pick, preferred_element_type=F32)
        w = jnp.broadcast_to(w[:, None, :], (IJ, 8, 512)).reshape(128, 512)
        wide[n * 128:(n + 1) * 128] = jnp.where(same, w, 0.0).astype(BF16)

    def stage1(n, ks):
        size = 256 if n < LT else 128 * ks

        def column(e2, carry):
            at = pl.ds(pl.multiple_of(e2 * 256, 256), 256)
            for r in range(3):
                lhs = left[r * 256:(r + 1) * 256, :] if n < LT else leftp[n - LT, 0:size, :]
                t = lax.dot_general(
                    lhs, right[n if n < LT else r, at, :],
                    (((1,), (1,)), ((), ())), preferred_element_type=F32,
                )
                for u in range(2):
                    tile[e2 * 2 + u, r * size:(r + 1) * size, :] = t[:, u * 128:(u + 1) * 128]
            return carry

        lax.fori_loop(0, CB // 2, column, 0)

    def stage2(n, ks):
        def rows(it, carry):
            his, los = [], []
            for u in range(2):
                base_ = (it * 2 + u) * 64
                s = jnp.concatenate(
                    [tile[e, pl.ds(pl.multiple_of(base_ + a * 8, 8), 8), :] for a in range(8) for e in range(CB)],
                    axis=0,
                )
                hi, lo = split(s)
                his.append(hi)
                los.append(lo)
            r = jnp.dot(wide[...], jnp.concatenate(his, axis=1), preferred_element_type=F32)
            q = jnp.dot(wide[0:128], jnp.concatenate(los, axis=1), preferred_element_type=F32)
            r = r[:128] + r[128:] + q
            for u in range(2):
                v = r[:, u * 128:(u + 1) * 128].reshape(IJ, 8, 128)
                if n < LT:
                    part[0, n, :, pl.ds(pl.multiple_of((it * 2 + u) * 8, 8), 8), :] = v
                else:
                    part[1 + lax.rem(it, ks), lax.div(it, ks), :, pl.ds((n - LT) * PC + u * 8, 8), :] = v
            return carry

        lax.fori_loop(0, 6 if n < LT else 3 * ks, rows, 0)

    base, away = core * 8, (1 - core) * 8
    sibling = dev(z, x, zl, y, 1 - core)
    y_left, y_right = dev(z, x, zl, yl, core), dev(z, x, zl, yr_, core)
    z_other = dev(z, x, 1 - zl, y, core)

    def spans(n, ks):
        if n < LT:
            return pl.ds(0, 1), pl.ds(n, 1), pl.ds(0, VB)
        return pl.ds(1, ks), pl.ds(0, LT), pl.ds((n - LT) * PC, PC)

    def blocks(n, ks):
        if n < LT:
            return [(0, n)], slice(0, VB)
        return [(k, l) for k in range(1, 1 + ks) for l in range(LT)], slice((n - LT) * PC, (n - LT) * PC + PC)

    def core_copy(n, ks):
        k, l, a = spans(n, ks)
        return remote(
            part.at[k, l, pl.ds(away, 8), a], cbuf.at[k, l, pl.ds(0, 8), a], cs.at[n], cr.at[n], sibling
        )

    def y_copies(n, ks):
        k, l, a = spans(n, ks)

        def one(c, y_, o, device):
            return remote(
                part.at[k, l, base + y_ * 2 + o, a], ybuf.at[c, k, l, a], ys.at[n, c], yr.at[n, c], device
            )

        return [
            one(0, y2, 0, y_right), one(1, yr_, 1, y_right), one(2, y2, 1, y_left),
            one(3, yl, 0, y_left), one(4, yr_, 0, y_right), one(5, yl, 1, y_left),
        ]

    def z_copy(n, ks):
        k, l, a = spans(n, ks)
        return remote(
            part.at[k, l, base + y * 2 + (1 - zl), a], zbuf.at[k, l, a], zs.at[n], zr.at[n], z_other
        )

    def y_step1(n, ks):
        core_copy(n, ks).wait_recv()
        kls, a = blocks(n, ks)

        def add(i, carry):
            for k, l in kls:
                part[k, l, base + i, a, :] = part[k, l, base + i, a, :] + cbuf[k, l, i, a, :]
            return carry

        lax.fori_loop(0, 8, add, 0)
        for c in y_copies(n, ks)[:4]:
            c.start()

    def y_step2(n, ks):
        copies = y_copies(n, ks)
        kls, a = blocks(n, ks)
        for first, i, then in ((0, base + yr_ * 2, 4), (2, base + yl * 2 + 1, 5)):
            copies[first].wait_recv()
            for k, l in kls:
                part[k, l, i, a, :] = part[k, l, i, a, :] + ybuf[first, k, l, a, :]
            copies[then].start()

    def y_step3(n, ks):
        copies = y_copies(n, ks)
        kls, a = blocks(n, ks)
        for o, pair in enumerate(((3, 4), (1, 5))):
            for c in pair:
                copies[c].wait_recv()
            i = base + y * 2 + o
            for k, l in kls:
                part[k, l, i, a, :] = part[k, l, i, a, :] + ybuf[pair[0], k, l, a, :] + ybuf[pair[1], k, l, a, :]
        z_copy(n, ks).start()

    def routes(k, op):
        if k == 0:
            zk = z
        elif k == 1:
            zk = jnp.where(z == 1, 3, jnp.where(z == 3, 2, 1))
        else:
            zk = jnp.where(z == 0, 3, 0)
        for xp in range(NX):
            src = piece.at[k, xp]
            valid = jnp.where(gt == 1, xp <= x, xp >= x) if k == 0 else jnp.bool_(True)
            here = xp == x

            def send(device, p, n):
                c = remote(src, rall.at[p], rs.at[k, xp, n], rr.at[p], device)
                if op == "start":
                    c.start()
                else:
                    c.wait_send()

            def keep(p):
                if op == "start":
                    pltpu.make_async_copy(src, rall.at[p], rr.at[p]).start()

            @pl.when(jnp.logical_and(valid, jnp.logical_not(here)))
            def _():
                send(dev(z, xp, zl, y, core), zk * 4 + x, 0)

            if k == 0:
                @pl.when(valid)
                def _():
                    keep(z * 4 + xp)
            else:
                @pl.when(here)
                def _():
                    keep(zk * 4 + x)

                send(dev(zk, x, zl, y, core), z * 4 + xp, 1)

    lane = lax.broadcasted_iota(jnp.int32, (24, 128), 1)
    tall = lax.broadcasted_iota(jnp.int32, (VB, 128), 1)

    def final(k):
        v = [part[k, l, base + y * 2 + zl] + zbuf[k, l] for l in range(LT)]
        for xp in range(NX):
            turn = [v[l] if l == xp else pltpu.roll(v[l], (l - xp) % 4 * 32, 1) for l in range(LT)]
            w = jnp.where(tall < 32, turn[0], jnp.where(tall < 64, turn[1], turn[2]))

            @pl.when(gt == 1)
            def _():
                square[0:VB] = w

            @pl.when(gt == 0)
            def _():
                square[...] = jnp.concatenate([w, jnp.zeros((128 - VB, 128), F32)], axis=0).T

            r = [square[pl.ds(n, 24, stride=4), :] for n in range(4)]
            p = piece.at[k, xp]
            p[pl.ds(0, 24, stride=3), :] = jnp.where(lane < 96, r[0], pltpu.roll(r[1], 96, 1))
            p[pl.ds(1, 24, stride=3), :] = jnp.where(lane < 64, pltpu.roll(r[1], 96, 1), pltpu.roll(r[2], 64, 1))
            p[pl.ds(2, 24, stride=3), :] = jnp.where(lane < 32, pltpu.roll(r[2], 64, 1), pltpu.roll(r[3], 32, 1))
        routes(k, "start")

    def gather(j):
        for d in range(2):
            g_from(j, d).wait_recv()
            g_forward(j, d).start()
            if j < 2:
                g_chunk(j + 1, d).start()
        convert_g(xl, j)
        convert_g(xr, j)

    def behind(j):
        for d in range(2):
            g_behind(j, d).wait_recv()
        convert_g(x2, j)

    gather(0)
    relay(0)
    behind(0)
    stage1(0, 1)
    stage2(0, 1)
    core_copy(0, 1).start()
    relay(1)
    gather(1)
    relay(2)
    behind(1)
    stage1(1, 1)
    y_step1(0, 1)
    stage2(1, 1)
    core_copy(1, 1).start()
    y_step2(0, 1)
    relay(3)
    gather(2)
    y_step1(1, 1)
    behind(2)
    stage1(2, 1)
    y_step2(1, 1)
    stage2(2, 1)
    core_copy(2, 1).start()
    y_step3(0, 1)
    relay(4)

    def rest(ks):
        for m in range(PN):
            n = LT + m
            if m == PN - 1:
                y_step1(n - 1, ks)
            for k in range(1, 1 + ks):
                if k == 1:
                    p_wait(1, m)
                else:
                    @pl.when(z == 2)
                    def _():
                        p_wait(2, m)
                convert_s(k, m)
            stage1(n, ks)
            if m < PN - 1:
                y_step1(n - 1, 1 if m == 0 else ks)
            else:
                y_step2(n - 1, ks)
            stage2(n, ks)
            core_copy(n, ks).start()
            if m == 1:
                relay(5)
            if m < PN - 1:
                y_step2(n - 1, 1 if m == 0 else ks)
            y_step3(n - 2, 1 if m < 2 else ks)
            if m == 2:
                for u in range(LT):
                    z_copy(u, 1).wait_recv()
                final(0)
        n = LT + PN - 1
        y_step1(n, ks)
        y_step3(n - 1, ks)
        y_step2(n, ks)
        y_step3(n, ks)
        for m in range(PN):
            z_copy(LT + m, ks).wait_recv()
        for k in range(1, 1 + ks):
            final(k)

    @pl.when(heavy)
    def _():
        rest(2)

    @pl.when(jnp.logical_not(heavy))
    def _():
        rest(1)

    for p in range(16):
        pltpu.make_async_copy(rall.at[p], rall.at[p], rr.at[p]).wait()
    for s in range(out.shape[0]):
        p = partners[0, s]
        out[s] = jnp.where(p >= 0, rall[jnp.maximum(p, 0)], 0.0)

    for j in range(LT):
        for d in range(2):
            g_chunk(j, d).wait_send()
            g_forward(j, d).wait_send()
    for m in range(PN):
        p_send(m).wait_send()
    for c in t_sends:
        c.wait_send()

    @pl.when(z == 1)
    def _():
        for m in range(PN):
            p_send_up(m).wait_send()

    @pl.when(ends)
    def _():
        for m in range(PN):
            p_relay(m).wait_send()

    def drain(n, ks):
        core_copy(n, ks).wait_send()
        for c in y_copies(n, ks):
            c.wait_send()
        z_copy(n, ks).wait_send()

    for n in range(LT):
        drain(n, 1)
    routes(0, "wait")
    routes(1, "wait")

    @pl.when(heavy)
    def _():
        for n in range(LT, LT + PN):
            drain(n, 2)
        routes(2, "wait")

    @pl.when(jnp.logical_not(heavy))
    def _():
        for n in range(LT, LT + PN):
            drain(n, 1)


def local(partners, cholesky, amplitudes):
    slots = partners.shape[1]
    chol = cholesky.reshape(VB, 2, CB, 2, 128).transpose(0, 1, 3, 2, 4)
    dma = pltpu.SemaphoreType.DMA
    res = pl.pallas_call(
        ladder,
        out_shape=jax.ShapeDtypeStruct((slots, 72, 128), F32),
        in_specs=[
            pl.BlockSpec(memory_space=pltpu.SMEM),
            pl.BlockSpec(memory_space=pl.ANY),
            pl.BlockSpec(memory_space=pltpu.VMEM),
        ],
        out_specs=pl.BlockSpec(memory_space=pltpu.VMEM),
        scratch_shapes=[
            pltpu.VMEM((NX, VB, 2, CB, 128), F32),
            pltpu.VMEM((3, VB, 2, CB, 128), F32),
            pltpu.VMEM((8, 128), F32),
            pltpu.VMEM((IJ, 8, 128), F32),
            pltpu.VMEM((256, 512), BF16),
            pltpu.VMEM((ROWS, 3 * QL), BF16),
            pltpu.VMEM((PN, 2 * PC * CB, 3 * QL), BF16),
            pltpu.VMEM((LT, CB * 128, 3 * QL), BF16),
            pltpu.VMEM((CB, ROWS, 128), F32),
            pltpu.VMEM((3, LT, IJ, VB, 128), F32),
            pltpu.VMEM((3, LT, 8, VB, 128), F32),
            pltpu.VMEM((6, 3, LT, VB, 128), F32),
            pltpu.VMEM((3, LT, VB, 128), F32),
            pltpu.VMEM((128, 128), F32),
            pltpu.VMEM((3, NX, 72, 128), F32),
            pltpu.VMEM((16, 72, 128), F32),
            dma((2,)),
            dma((3, 4)), dma((3, 4)),
            dma((3, PN)), dma((3, PN)),
            dma((15,)), dma((16,)),
            dma((9,)), dma((9,)),
            dma((9, 6)), dma((9, 6)),
            dma((9,)), dma((9,)),
            dma((3, NX, 2)), dma((16,)),
        ],
        compiler_params=pltpu.CompilerParams(
            collective_id=0, has_side_effects=True, vmem_limit_bytes=56 * 1024 * 1024
        ),
    )(partners, chol, amplitudes)
    return res.reshape(slots, 1, VB * VB)


def solution(mesh):
    return jax.shard_map(
        local,
        mesh=mesh,
        in_specs=(P("ab", None), P("ab", None, "ij"), P("ij", None)),
        out_specs=P("ab", "ij", None),
        check_vma=False,
    )
```

```python
import jax
import jax.numpy as jnp
from jax import lax
from jax.experimental import pallas as pl
from jax.experimental.pallas import tpu as pltpu
from jax.sharding import PartitionSpec as P

MESH = pl.DeviceIdType.MESH
F32 = jnp.float32
BF16 = jnp.bfloat16
VB = 96
CB = 8
QL = 256
ROWS = VB * CB
NX = 4
LT = 3
CH = 32
PC = 16
PN = 6
IJ = 16


def split(v):
    hi = v.astype(BF16)
    lo = (v - hi.astype(F32)).astype(BF16)
    return hi, lo


def ladder(
    partners, chol, amp, out,
    gbuf, sbuf, abuf, tbuf, wide, left, leftp, right, tile, part, cbuf, ybuf, zbuf, square, piece, rall,
    lsem, gs, gr, ps, pr, ts, tr, cs, cr, ys, yr, zs, zr, rs, rr,
):
    ab = lax.axis_index("ab")
    ij = lax.axis_index("ij")
    z, x = lax.div(ab, 4), lax.rem(ab, 4)
    zl, y, core = lax.div(ij, 8), lax.rem(lax.div(ij, 2), 4), lax.rem(ij, 2)

    def dev(z_, x_, zl_, y_, core_):
        return (z_ * 4 + x_, zl_ * 8 + y_ * 2 + core_)

    def mod4(v):
        return lax.rem(v + 8, 4)

    gt = jnp.where(z < 2, 1, 0)
    xl, xr, x2 = mod4(x - 1), mod4(x + 1), mod4(x + 2)
    yl, yr_, y2 = mod4(y - 1), mod4(y + 1), mod4(y + 2)
    heavy = lax.rem(z, 2) == 0
    ends = jnp.logical_or(z == 0, z == 3)
    slot = core * 8 + y * 2 + zl

    barrier = pltpu.get_barrier_semaphore()
    peers = [(ab, lax.rem(ij + n, 16)) for n in range(1, 16)]
    for n in range(1, 4):
        peers.append(dev(z, mod4(x + n), zl, y, core))
        peers.append(dev(mod4(z + n), x, zl, y, core))
    for peer in peers:
        pl.semaphore_signal(barrier, inc=1, device_id=peer, device_id_type=MESH)
    own_g = chol.at[:, gt]
    local_g = pltpu.make_async_copy(own_g, gbuf.at[x], lsem.at[0])
    local_s = pltpu.make_async_copy(chol.at[:, 1 - gt], sbuf.at[0], lsem.at[1])
    local_g.start()
    local_s.start()
    row = jnp.concatenate([amp[...], jnp.zeros((1, 64), F32)], axis=1)
    abuf[...] = jnp.broadcast_to(row, (8, 128))
    pl.semaphore_wait(barrier, len(peers))

    def remote(src, dst, send, recv, device):
        return pltpu.make_async_remote_copy(
            src_ref=src, dst_ref=dst, send_sem=send, recv_sem=recv, device_id=device, device_id_type=MESH
        )

    to_right, to_left = dev(z, xr, zl, y, core), dev(z, xl, zl, y, core)

    def g_chunk(j, d):
        return remote(
            chol.at[pl.ds(j * CH, CH), gt], gbuf.at[x, pl.ds(j * CH, CH)], gs.at[j, d], gr.at[j, d],
            (to_right, to_left)[d],
        )

    def g_from(j, d):
        at = gbuf.at[(xl, xr)[d], pl.ds(j * CH, CH)]
        return remote(at, at, gs.at[j, d], gr.at[j, d], (to_right, to_left)[d])

    def g_forward(j, d):
        at = gbuf.at[(xl, xr)[d], pl.ds(j * CH + d * 16, 16)]
        return remote(at, at, gs.at[j, 2 + d], gr.at[j, 2 + d], (to_right, to_left)[d])

    def g_behind(j, d):
        at = gbuf.at[x2, pl.ds(j * CH + d * 16, 16)]
        return remote(at, at, gs.at[j, 2 + d], gr.at[j, 2 + d], (to_right, to_left)[d])

    def p_send(m):
        rows = pl.ds(m * PC, PC)
        to = jnp.where(ends, 2, 1)
        return remote(
            chol.at[rows, 1 - lax.rem(z, 2)], sbuf.at[to, rows], ps.at[0, m], pr.at[to, m],
            dev(3 * (1 - lax.rem(z, 2)), x, zl, y, core),
        )

    def p_send_up(m):
        rows = pl.ds(m * PC, PC)
        return remote(
            chol.at[rows, 1], sbuf.at[1, rows], ps.at[1, m], pr.at[1, m], dev(2, x, zl, y, core)
        )

    def p_relay(m):
        rows = pl.ds(m * PC, PC)
        to = jnp.where(z == 0, 1, 2)
        return remote(
            sbuf.at[2, rows], sbuf.at[to, rows], ps.at[2, m], pr.at[to, m], dev(to, x, zl, y, core)
        )

    def p_wait(k, m):
        at = sbuf.at[k, pl.ds(m * PC, PC)]
        remote(at, at, ps.at[0, m], pr.at[k, m], to_right).wait_recv()

    for d in range(2):
        g_chunk(0, d).start()
    def p_start(m):
        p_send(m).start()

        @pl.when(z == 1)
        def _():
            p_send_up(m).start()

    def pump(m):
        p_send(m).wait_send()

        @pl.when(z == 1)
        def _():
            p_send_up(m).wait_send()

        if m + 2 < PN:
            p_start(m + 2)

        @pl.when(ends)
        def _():
            p_wait(2, m)
            p_relay(m).start()

    p_start(0)
    p_start(1)
    t_sends = [
        remote(abuf, tbuf.at[slot], ts.at[n - 1], tr.at[slot], (ab, lax.rem(ij + n, 16)))
        for n in range(1, 16)
    ]
    for c in t_sends:
        c.start()
    tbuf[slot] = abuf[...]

    gview = gbuf.reshape(NX, VB * 2 * CB, 128)

    def convert_g(n, j):
        for e in range(CB):
            v = jnp.concatenate(
                [gview[n, pl.ds(j * CH * 16 + h * CB + e, CH, stride=2 * CB), :] for h in range(2)], axis=1
            )
            hi, lo = split(v)
            at = pl.ds(pl.multiple_of(e * 128 + n * CH, CH), CH)
            right[j, at, 0:QL] = hi
            right[j, at, QL:2 * QL] = lo
            right[j, at, 2 * QL:3 * QL] = hi

    def convert_s(k, m):
        for h in range(2):
            v = sbuf[k, pl.ds(m * PC, PC), h].reshape(PC * CB, 128)
            hi, lo = split(v)
            to = left.at[pl.ds(m * PC * CB, PC * CB)] if k == 0 else leftp.at[m, pl.ds((k - 1) * PC * CB, PC * CB)]
            to[:, h * 128:h * 128 + 128] = hi
            to[:, QL + h * 128:QL + h * 128 + 128] = hi
            to[:, 2 * QL + h * 128:2 * QL + h * 128 + 128] = lo

    local_g.wait()
    local_s.wait()
    for j in range(LT):
        convert_g(x, j)
    for m in range(PN):
        convert_s(0, m)

    for n in range(1, 16):
        peer = lax.rem(ij + n, 16)
        other = lax.rem(peer, 2) * 8 + lax.rem(lax.div(peer, 2), 4) * 2 + lax.div(peer, 8)
        remote(abuf, tbuf.at[other], ts.at[0], tr.at[other], (ab, peer)).wait_recv()
    source = lax.broadcasted_iota(jnp.int32, (128, 512), 0)
    target = lax.rem(lax.broadcasted_iota(jnp.int32, (128, 512), 1), 64)
    turned = lax.rem(target, 8) * 8 + lax.div(target, 8)
    pick = jnp.where(source == jnp.where(gt == 1, turned, target), 1.0, 0.0).astype(BF16)
    same = lax.rem(lax.broadcasted_iota(jnp.int32, (128, 512), 0), 8) == lax.div(
        lax.broadcasted_iota(jnp.int32, (128, 512), 1), 64
    )
    for n, v in enumerate(split(tbuf[:, 0, :])):
        w = jnp.dot(v, pick, preferred_element_type=F32)
        w = jnp.broadcast_to(w[:, None, :], (IJ, 8, 512)).reshape(128, 512)
        wide[n * 128:(n + 1) * 128] = jnp.where(same, w, 0.0).astype(BF16)

    units = [("own", 0), ("own", 1), ("half", 0), ("half", 1), ("own", 2), ("half", 2)]
    units += [("rows", m) for m in range(3, PN)]

    def stage1(n, ks):
        kind, v = units[n]
        size = 256 if kind == "own" else 128 * ks

        def column(e2, carry):
            at = pl.ds(pl.multiple_of(e2 * 256, 256), 256)
            for r in range(3):
                if kind == "own":
                    lhs = left[r * 256:(r + 1) * 256, :]
                else:
                    lhs = leftp[r if kind == "half" else v, 0:size, :]
                t = lax.dot_general(
                    lhs, right[r if kind == "rows" else v, at, :],
                    (((1,), (1,)), ((), ())), preferred_element_type=F32,
                )
                for u in range(2):
                    tile[e2 * 2 + u, r * size:(r + 1) * size, :] = t[:, u * 128:(u + 1) * 128]
            return carry

        lax.fori_loop(0, CB // 2, column, 0)

    def stage2(n, ks):
        kind, w = units[n]

        def rows(it, carry):
            his, los = [], []
            for u in range(2):
                base_ = (it * 2 + u) * 64
                s = jnp.concatenate(
                    [tile[e, pl.ds(pl.multiple_of(base_ + a * 8, 8), 8), :] for a in range(8) for e in range(CB)],
                    axis=0,
                )
                hi, lo = split(s)
                his.append(hi)
                los.append(lo)
            r = jnp.dot(wide[...], jnp.concatenate(his, axis=1), preferred_element_type=F32)
            q = jnp.dot(wide[0:128], jnp.concatenate(los, axis=1), preferred_element_type=F32)
            r = r[:128] + r[128:] + q
            for u in range(2):
                v = r[:, u * 128:(u + 1) * 128].reshape(IJ, 8, 128)
                if kind == "own":
                    part[0, w, :, pl.ds(pl.multiple_of((it * 2 + u) * 8, 8), 8), :] = v
                elif kind == "half":
                    at = pl.multiple_of(lax.div(it, ks) * PC + u * 8, 8)
                    part[1 + lax.rem(it, ks), w, :, pl.ds(at, 8), :] = v
                else:
                    part[1 + lax.rem(it, ks), lax.div(it, ks), :, pl.ds(w * PC + u * 8, 8), :] = v
            return carry

        lax.fori_loop(0, 6 if kind == "own" else 3 * ks, rows, 0)

    base, away = core * 8, (1 - core) * 8
    sibling = dev(z, x, zl, y, 1 - core)
    y_left, y_right = dev(z, x, zl, yl, core), dev(z, x, zl, yr_, core)
    z_other = dev(z, x, 1 - zl, y, core)

    def reach(n):
        kind, v = units[n]
        return {"own": (v, 1, 0, VB), "half": (v, 1, 0, 3 * PC), "rows": (0, LT, v * PC, PC)}[kind]

    def spans(n, ks):
        l, ln, a, an = reach(n)
        return pl.ds(0, 1) if units[n][0] == "own" else pl.ds(1, ks), pl.ds(l, ln), pl.ds(a, an)

    def blocks(n, ks):
        l, ln, a, an = reach(n)
        ks_ = [0] if units[n][0] == "own" else range(1, 1 + ks)
        return [(k, l_) for k in ks_ for l_ in range(l, l + ln)], slice(a, a + an)

    def core_copy(n, ks):
        k, l, a = spans(n, ks)
        return remote(
            part.at[k, l, pl.ds(away, 8), a], cbuf.at[k, l, pl.ds(0, 8), a], cs.at[n], cr.at[n], sibling
        )

    def y_copies(n, ks):
        k, l, a = spans(n, ks)

        def one(c, y_, o, device):
            return remote(
                part.at[k, l, base + y_ * 2 + o, a], ybuf.at[c, k, l, a], ys.at[n, c], yr.at[n, c], device
            )

        return [
            one(0, y2, 0, y_right), one(1, yr_, 1, y_right), one(2, y2, 1, y_left),
            one(3, yl, 0, y_left), one(4, yr_, 0, y_right), one(5, yl, 1, y_left),
        ]

    def z_copy(n, ks):
        k, l, a = spans(n, ks)
        return remote(
            part.at[k, l, base + y * 2 + (1 - zl), a], zbuf.at[k, l, a], zs.at[n], zr.at[n], z_other
        )

    def y_step1(n, ks):
        core_copy(n, ks).wait_recv()
        kls, a = blocks(n, ks)

        def add(i, carry):
            for k, l in kls:
                part[k, l, base + i, a, :] = part[k, l, base + i, a, :] + cbuf[k, l, i, a, :]
            return carry

        lax.fori_loop(0, 8, add, 0)
        for c in y_copies(n, ks)[:4]:
            c.start()

    def y_step2(n, ks):
        copies = y_copies(n, ks)
        kls, a = blocks(n, ks)
        for first, i, then in ((0, base + yr_ * 2, 4), (2, base + yl * 2 + 1, 5)):
            copies[first].wait_recv()
            for k, l in kls:
                part[k, l, i, a, :] = part[k, l, i, a, :] + ybuf[first, k, l, a, :]
            copies[then].start()

    def y_step3(n, ks):
        copies = y_copies(n, ks)
        kls, a = blocks(n, ks)
        for o, pair in enumerate(((3, 4), (1, 5))):
            for c in pair:
                copies[c].wait_recv()
            i = base + y * 2 + o
            for k, l in kls:
                part[k, l, i, a, :] = part[k, l, i, a, :] + ybuf[pair[0], k, l, a, :] + ybuf[pair[1], k, l, a, :]
        z_copy(n, ks).start()

    def routes(k, op):
        if k == 0:
            zk = z
        elif k == 1:
            zk = jnp.where(z == 1, 3, jnp.where(z == 3, 2, 1))
        else:
            zk = jnp.where(z == 0, 3, 0)
        for xp in range(NX):
            src = piece.at[k, xp]
            valid = jnp.where(gt == 1, xp <= x, xp >= x) if k == 0 else jnp.bool_(True)
            here = xp == x

            def send(device, p, n):
                c = remote(src, rall.at[p], rs.at[k, xp, n], rr.at[p], device)
                if op == "start":
                    c.start()
                else:
                    c.wait_send()

            def keep(p):
                if op == "start":
                    pltpu.make_async_copy(src, rall.at[p], rr.at[p]).start()

            @pl.when(jnp.logical_and(valid, jnp.logical_not(here)))
            def _():
                send(dev(z, xp, zl, y, core), zk * 4 + x, 0)

            if k == 0:
                @pl.when(valid)
                def _():
                    keep(z * 4 + xp)
            else:
                @pl.when(here)
                def _():
                    keep(zk * 4 + x)

                send(dev(zk, x, zl, y, core), z * 4 + xp, 1)

    lane = lax.broadcasted_iota(jnp.int32, (24, 128), 1)
    tall = lax.broadcasted_iota(jnp.int32, (VB, 128), 1)

    def final(k):
        v = [part[k, l, base + y * 2 + zl] + zbuf[k, l] for l in range(LT)]
        for xp in range(NX):
            turn = [v[l] if l == xp else pltpu.roll(v[l], (l - xp) % 4 * 32, 1) for l in range(LT)]
            w = jnp.where(tall < 32, turn[0], jnp.where(tall < 64, turn[1], turn[2]))

            @pl.when(gt == 1)
            def _():
                square[0:VB] = w

            @pl.when(gt == 0)
            def _():
                square[...] = jnp.concatenate([w, jnp.zeros((128 - VB, 128), F32)], axis=0).T

            r = [square[pl.ds(n, 24, stride=4), :] for n in range(4)]
            p = piece.at[k, xp]
            p[pl.ds(0, 24, stride=3), :] = jnp.where(lane < 96, r[0], pltpu.roll(r[1], 96, 1))
            p[pl.ds(1, 24, stride=3), :] = jnp.where(lane < 64, pltpu.roll(r[1], 96, 1), pltpu.roll(r[2], 64, 1))
            p[pl.ds(2, 24, stride=3), :] = jnp.where(lane < 32, pltpu.roll(r[2], 64, 1), pltpu.roll(r[3], 32, 1))
        routes(k, "start")

    def gather(j):
        for d in range(2):
            g_from(j, d).wait_recv()
            g_forward(j, d).start()
            if j < 2:
                g_chunk(j + 1, d).start()
        convert_g(xl, j)
        convert_g(xr, j)

    def behind(j):
        for d in range(2):
            g_behind(j, d).wait_recv()
        convert_g(x2, j)

    gather(0)
    pump(0)
    behind(0)
    stage1(0, 1)
    stage2(0, 1)
    core_copy(0, 1).start()
    pump(1)
    y_step1(0, 1)
    gather(1)
    y_step2(0, 1)
    behind(1)
    pump(2)
    stage1(1, 1)
    stage2(1, 1)
    core_copy(1, 1).start()
    y_step3(0, 1)

    def fetch(ks, m):
        for k in range(1, 1 + ks):
            if k == 1:
                p_wait(1, m)
            else:
                @pl.when(z == 2)
                def _():
                    p_wait(2, m)
            convert_s(k, m)

    def rest(ks):
        gather(2)
        y_step1(1, 1)
        pump(3)
        for m in range(3):
            fetch(ks, m)
        last = len(units) - 1
        for n in range(2, last + 1):
            if n == last:
                y_step2(n - 2, ks)
                y_step1(n - 1, ks)
            if units[n][0] == "rows":
                fetch(ks, units[n][1])
            stage1(n, ks)
            if 2 < n < last:
                y_step2(n - 2, ks)
                y_step1(n - 1, ks)
            stage2(n, ks)
            core_copy(n, ks).start()
            if n > 3:
                y_step3(n - 3, ks)
            if n == 3:
                behind(2)
                pump(4)
            if n == 6:
                pump(5)
        y_step2(last - 1, ks)
        y_step1(last, ks)
        y_step3(last - 2, ks)
        for u in (0, 1, 4):
            z_copy(u, ks).wait_recv()
        final(0)
        y_step3(last - 1, ks)
        y_step2(last, ks)
        y_step3(last, ks)
        for n in range(2, last + 1):
            if n != 4:
                z_copy(n, ks).wait_recv()
        for k in range(1, 1 + ks):
            final(k)

    @pl.when(heavy)
    def _():
        rest(2)

    @pl.when(jnp.logical_not(heavy))
    def _():
        rest(1)

    for p in range(16):
        pltpu.make_async_copy(rall.at[p], rall.at[p], rr.at[p]).wait()
    for s in range(out.shape[0]):
        p = partners[0, s]
        out[s] = jnp.where(p >= 0, rall[jnp.maximum(p, 0)], 0.0)

    for j in range(LT):
        for d in range(2):
            g_chunk(j, d).wait_send()
            g_forward(j, d).wait_send()
    for c in t_sends:
        c.wait_send()

    @pl.when(ends)
    def _():
        for m in range(PN):
            p_relay(m).wait_send()

    def drain(n, ks):
        core_copy(n, ks).wait_send()
        for c in y_copies(n, ks):
            c.wait_send()
        z_copy(n, ks).wait_send()

    routes(0, "wait")
    routes(1, "wait")

    @pl.when(heavy)
    def _():
        for n in range(len(units)):
            drain(n, 2)
        routes(2, "wait")

    @pl.when(jnp.logical_not(heavy))
    def _():
        for n in range(len(units)):
            drain(n, 1)


def local(partners, cholesky, amplitudes):
    slots = partners.shape[1]
    chol = cholesky.reshape(VB, 2, CB, 2, 128).transpose(0, 1, 3, 2, 4)
    dma = pltpu.SemaphoreType.DMA
    res = pl.pallas_call(
        ladder,
        out_shape=jax.ShapeDtypeStruct((slots, 72, 128), F32),
        in_specs=[
            pl.BlockSpec(memory_space=pltpu.SMEM),
            pl.BlockSpec(memory_space=pl.ANY),
            pl.BlockSpec(memory_space=pltpu.VMEM),
        ],
        out_specs=pl.BlockSpec(memory_space=pltpu.VMEM),
        scratch_shapes=[
            pltpu.VMEM((NX, VB, 2, CB, 128), F32),
            pltpu.VMEM((3, VB, 2, CB, 128), F32),
            pltpu.VMEM((8, 128), F32),
            pltpu.VMEM((IJ, 8, 128), F32),
            pltpu.VMEM((256, 512), BF16),
            pltpu.VMEM((ROWS, 3 * QL), BF16),
            pltpu.VMEM((PN, 2 * PC * CB, 3 * QL), BF16),
            pltpu.VMEM((LT, CB * 128, 3 * QL), BF16),
            pltpu.VMEM((CB, ROWS, 128), F32),
            pltpu.VMEM((3, LT, IJ, VB, 128), F32),
            pltpu.VMEM((3, LT, 8, VB, 128), F32),
            pltpu.VMEM((6, 3, LT, VB, 128), F32),
            pltpu.VMEM((3, LT, VB, 128), F32),
            pltpu.VMEM((128, 128), F32),
            pltpu.VMEM((3, NX, 72, 128), F32),
            pltpu.VMEM((16, 72, 128), F32),
            dma((2,)),
            dma((3, 4)), dma((3, 4)),
            dma((3, PN)), dma((3, PN)),
            dma((15,)), dma((16,)),
            dma((9,)), dma((9,)),
            dma((9, 6)), dma((9, 6)),
            dma((9,)), dma((9,)),
            dma((3, NX, 2)), dma((16,)),
        ],
        compiler_params=pltpu.CompilerParams(
            collective_id=0, has_side_effects=True, vmem_limit_bytes=56 * 1024 * 1024
        ),
    )(partners, chol, amplitudes)
    return res.reshape(slots, 1, VB * VB)


def solution(mesh):
    return jax.shard_map(
        local,
        mesh=mesh,
        in_specs=(P("ab", None), P("ab", None, "ij"), P("ij", None)),
        out_specs=P("ab", "ij", None),
        check_vma=False,
    )
```

```python
import jax
import jax.numpy as jnp
from jax import lax
from jax.experimental import pallas as pl
from jax.experimental.pallas import tpu as pltpu
from jax.sharding import PartitionSpec as P

MESH = pl.DeviceIdType.MESH
F32 = jnp.float32
BF16 = jnp.bfloat16
VB = 96
CB = 8
QL = 256
ROWS = VB * CB
NX = 4
LT = 3
CH = 32
PC = 16
PN = 6
IJ = 16


def split(v):
    hi = v.astype(BF16)
    lo = (v - hi.astype(F32)).astype(BF16)
    return hi, lo


def ladder(
    partners, chol, amp, out,
    gbuf, sbuf, abuf, tbuf, wide, left, leftp, right, tile, part, cbuf, ybuf, zbuf, square, piece, rall,
    lsem, gs, gr, ps, pr, ts, tr, cs, cr, ys, yr, zs, zr, rs, rr,
):
    ab = lax.axis_index("ab")
    ij = lax.axis_index("ij")
    z, x = lax.div(ab, 4), lax.rem(ab, 4)
    zl, y, core = lax.div(ij, 8), lax.rem(lax.div(ij, 2), 4), lax.rem(ij, 2)

    def dev(z_, x_, zl_, y_, core_):
        return (z_ * 4 + x_, zl_ * 8 + y_ * 2 + core_)

    def mod4(v):
        return lax.rem(v + 8, 4)

    gt = jnp.where(z < 2, 1, 0)
    xl, xr, x2 = mod4(x - 1), mod4(x + 1), mod4(x + 2)
    yl, yr_, y2 = mod4(y - 1), mod4(y + 1), mod4(y + 2)
    heavy = lax.rem(z, 2) == 0
    ends = jnp.logical_or(z == 0, z == 3)
    slot = core * 8 + y * 2 + zl

    barrier = pltpu.get_barrier_semaphore()
    peers = [(ab, lax.rem(ij + n, 16)) for n in range(1, 16)]
    for n in range(1, 4):
        peers.append(dev(z, mod4(x + n), zl, y, core))
        peers.append(dev(mod4(z + n), x, zl, y, core))
    for peer in peers:
        pl.semaphore_signal(barrier, inc=1, device_id=peer, device_id_type=MESH)
    own_g = chol.at[:, gt]
    local_g = pltpu.make_async_copy(own_g, gbuf.at[x], lsem.at[0])
    local_s = pltpu.make_async_copy(chol.at[:, 1 - gt], sbuf.at[0], lsem.at[1])
    local_g.start()
    local_s.start()
    row = jnp.concatenate([amp[...], jnp.zeros((1, 64), F32)], axis=1)
    abuf[...] = jnp.broadcast_to(row, (8, 128))
    pl.semaphore_wait(barrier, len(peers))

    def remote(src, dst, send, recv, device):
        return pltpu.make_async_remote_copy(
            src_ref=src, dst_ref=dst, send_sem=send, recv_sem=recv, device_id=device, device_id_type=MESH
        )

    to_right, to_left = dev(z, xr, zl, y, core), dev(z, xl, zl, y, core)

    def g_chunk(j, d):
        return remote(
            chol.at[pl.ds(j * CH, CH), gt], gbuf.at[x, pl.ds(j * CH, CH)], gs.at[j, d], gr.at[j, d],
            (to_right, to_left)[d],
        )

    def g_from(j, d):
        at = gbuf.at[(xl, xr)[d], pl.ds(j * CH, CH)]
        return remote(at, at, gs.at[j, d], gr.at[j, d], (to_right, to_left)[d])

    def g_forward(j, d):
        at = gbuf.at[(xl, xr)[d], pl.ds(j * CH + d * 16, 16)]
        return remote(at, at, gs.at[j, 2 + d], gr.at[j, 2 + d], (to_right, to_left)[d])

    def g_behind(j, d):
        at = gbuf.at[x2, pl.ds(j * CH + d * 16, 16)]
        return remote(at, at, gs.at[j, 2 + d], gr.at[j, 2 + d], (to_right, to_left)[d])

    def p_send(m):
        rows = pl.ds(m * PC, PC)
        to = jnp.where(ends, 2, 1)
        return remote(
            chol.at[rows, 1 - lax.rem(z, 2)], sbuf.at[to, rows], ps.at[0, m], pr.at[to, m],
            dev(3 * (1 - lax.rem(z, 2)), x, zl, y, core),
        )

    def p_send_up(m):
        rows = pl.ds(m * PC, PC)
        return remote(
            chol.at[rows, 1], sbuf.at[1, rows], ps.at[1, m], pr.at[1, m], dev(2, x, zl, y, core)
        )

    def p_relay(m):
        rows = pl.ds(m * PC, PC)
        to = jnp.where(z == 0, 1, 2)
        return remote(
            sbuf.at[2, rows], sbuf.at[to, rows], ps.at[2, m], pr.at[to, m], dev(to, x, zl, y, core)
        )

    def p_wait(k, m):
        at = sbuf.at[k, pl.ds(m * PC, PC)]
        remote(at, at, ps.at[0, m], pr.at[k, m], to_right).wait_recv()

    for d in range(2):
        g_chunk(0, d).start()
    def p_start(m):
        p_send(m).start()

        @pl.when(z == 1)
        def _():
            p_send_up(m).start()

    def pump(m):
        p_send(m).wait_send()

        @pl.when(z == 1)
        def _():
            p_send_up(m).wait_send()

        if m + 2 < PN:
            p_start(m + 2)

        @pl.when(ends)
        def _():
            p_wait(2, m)
            p_relay(m).start()

    p_start(0)
    p_start(1)
    t_sends = [
        remote(abuf, tbuf.at[slot], ts.at[n - 1], tr.at[slot], (ab, lax.rem(ij + n, 16)))
        for n in range(1, 16)
    ]
    for c in t_sends:
        c.start()
    tbuf[slot] = abuf[...]

    gview = gbuf.reshape(NX, VB * 2 * CB, 128)

    def convert_g(n, j):
        for e in range(CB):
            v = jnp.concatenate(
                [gview[n, pl.ds(j * CH * 16 + h * CB + e, CH, stride=2 * CB), :] for h in range(2)], axis=1
            )
            hi, lo = split(v)
            at = pl.ds(pl.multiple_of(e * 128 + n * CH, CH), CH)
            right[j, at, 0:QL] = hi
            right[j, at, QL:2 * QL] = lo
            right[j, at, 2 * QL:3 * QL] = hi

    def convert_s(k, m):
        for h in range(2):
            v = sbuf[k, pl.ds(m * PC, PC), h].reshape(PC * CB, 128)
            hi, lo = split(v)
            to = left.at[pl.ds(m * PC * CB, PC * CB)] if k == 0 else leftp.at[m, pl.ds((k - 1) * PC * CB, PC * CB)]
            to[:, h * 128:h * 128 + 128] = hi
            to[:, QL + h * 128:QL + h * 128 + 128] = hi
            to[:, 2 * QL + h * 128:2 * QL + h * 128 + 128] = lo

    local_g.wait()
    local_s.wait()
    for j in range(LT):
        convert_g(x, j)
    for m in range(PN):
        convert_s(0, m)

    for n in range(1, 16):
        peer = lax.rem(ij + n, 16)
        other = lax.rem(peer, 2) * 8 + lax.rem(lax.div(peer, 2), 4) * 2 + lax.div(peer, 8)
        remote(abuf, tbuf.at[other], ts.at[0], tr.at[other], (ab, peer)).wait_recv()
    source = lax.broadcasted_iota(jnp.int32, (128, 512), 0)
    target = lax.broadcasted_iota(jnp.int32, (128, 512), 1)
    outer, inner = lax.div(target, 64), lax.rem(target, 8)
    pick = jnp.where(source == jnp.where(gt == 1, inner * 8 + outer, outer * 8 + inner), 1.0, 0.0).astype(BF16)
    same = lax.rem(source, 8) == lax.rem(lax.div(target, 8), 8)
    for n, v in enumerate(split(tbuf[:, 0, :])):
        w = jnp.dot(v, pick, preferred_element_type=F32)
        w = jnp.broadcast_to(w[:, None, :], (IJ, 8, 512)).reshape(128, 512)
        wide[n * 128:(n + 1) * 128] = jnp.where(same, w, 0.0).astype(BF16)

    units = [("own", 0), ("own", 1), ("half", 0), ("half", 1), ("own", 2), ("half", 2)]
    units += [("rows", m) for m in range(3, PN)]

    def stage1(n, ks):
        kind, v = units[n]
        size = 256 if kind == "own" else 128 * ks

        def column(en, carry):
            at = pl.ds(en * 256, 256) if isinstance(en, int) else pl.ds(pl.multiple_of(en * 256, 256), 256)
            for r in range(3):
                if kind == "own":
                    lhs = left[r * 256:(r + 1) * 256, :]
                else:
                    lhs = leftp[r if kind == "half" else v, 0:size, :]
                t = lax.dot_general(
                    lhs, right[r if kind == "rows" else v, at, :],
                    (((1,), (1,)), ((), ())), preferred_element_type=F32,
                )
                hi, lo = split(t)
                for u in range(256 // 128):
                    tile[0, en * 2 + u, r * size:(r + 1) * size, :] = hi[:, u * 128:(u + 1) * 128]
                    tile[1, en * 2 + u, r * size:(r + 1) * size, :] = lo[:, u * 128:(u + 1) * 128]
            return carry

        for en in range(CB * 128 // 256):
            column(en, 0)

    def stage2(n, ks):
        kind, w = units[n]

        many = 4 if kind == "own" else 2 * ks

        def rows(it, carry):
            cols = []
            for h in range(2):
                at = [(it * many + u) * 64 for u in range(many)]
                cols.append(
                    jnp.concatenate(
                        [jnp.concatenate([tile[h, e, pl.ds(b, 64), :] for e in range(CB)], axis=0) for b in at], axis=1
                    )
                )
            r = jnp.dot(wide[...], cols[0], preferred_element_type=F32)
            q = jnp.dot(wide[0:128], cols[1], preferred_element_type=F32)
            r = r[:128] + r[128:] + q
            for u in range(many):
                v = r[:, u * 128:(u + 1) * 128].reshape(IJ, 8, 128)
                if kind == "own":
                    part[0, w, :, pl.ds((it * many + u) * 8, 8), :] = v
                elif kind == "half":
                    part[1 + u // 2, w, :, pl.ds(it * PC + u % 2 * 8, 8), :] = v
                else:
                    part[1 + u // 2, it, :, pl.ds(w * PC + u % 2 * 8, 8), :] = v
            return carry

        for it in range(3):
            rows(it, 0)

    base, away = core * 8, (1 - core) * 8
    sibling = dev(z, x, zl, y, 1 - core)
    y_left, y_right = dev(z, x, zl, yl, core), dev(z, x, zl, yr_, core)
    z_other = dev(z, x, 1 - zl, y, core)

    def reach(n):
        kind, v = units[n]
        return {"own": (v, 1, 0, VB), "half": (v, 1, 0, 3 * PC), "rows": (0, LT, v * PC, PC)}[kind]

    def spans(n, ks):
        l, ln, a, an = reach(n)
        return pl.ds(0, 1) if units[n][0] == "own" else pl.ds(1, ks), pl.ds(l, ln), pl.ds(a, an)

    def blocks(n, ks):
        l, ln, a, an = reach(n)
        ks_ = [0] if units[n][0] == "own" else range(1, 1 + ks)
        return [(k, l_) for k in ks_ for l_ in range(l, l + ln)], slice(a, a + an)

    def core_copy(n, ks):
        k, l, a = spans(n, ks)
        return remote(
            part.at[k, l, pl.ds(away, 8), a], cbuf.at[k, l, pl.ds(0, 8), a], cs.at[n], cr.at[n], sibling
        )

    def y_copies(n, ks):
        k, l, a = spans(n, ks)

        def one(c, y_, o, device):
            return remote(
                part.at[k, l, base + y_ * 2 + o, a], ybuf.at[c, k, l, a], ys.at[n, c], yr.at[n, c], device
            )

        return [
            one(0, y2, 0, y_right), one(1, yr_, 1, y_right), one(2, y2, 1, y_left),
            one(3, yl, 0, y_left), one(4, yr_, 0, y_right), one(5, yl, 1, y_left),
        ]

    def z_copy(n, ks):
        k, l, a = spans(n, ks)
        return remote(
            part.at[k, l, base + y * 2 + (1 - zl), a], zbuf.at[k, l, a], zs.at[n], zr.at[n], z_other
        )

    def y_step1(n, ks):
        core_copy(n, ks).wait_recv()
        kls, a = blocks(n, ks)

        def add(i, carry):
            for k, l in kls:
                part[k, l, base + i, a, :] = part[k, l, base + i, a, :] + cbuf[k, l, i, a, :]
            return carry

        lax.fori_loop(0, 8, add, 0)
        for c in y_copies(n, ks)[:4]:
            c.start()

    def y_step2(n, ks):
        copies = y_copies(n, ks)
        kls, a = blocks(n, ks)
        for first, i, then in ((0, base + yr_ * 2, 4), (2, base + yl * 2 + 1, 5)):
            copies[first].wait_recv()
            for k, l in kls:
                part[k, l, i, a, :] = part[k, l, i, a, :] + ybuf[first, k, l, a, :]
            copies[then].start()

    def y_step3(n, ks):
        copies = y_copies(n, ks)
        kls, a = blocks(n, ks)
        for o, pair in enumerate(((3, 4), (1, 5))):
            for c in pair:
                copies[c].wait_recv()
            i = base + y * 2 + o
            for k, l in kls:
                part[k, l, i, a, :] = part[k, l, i, a, :] + ybuf[pair[0], k, l, a, :] + ybuf[pair[1], k, l, a, :]
        z_copy(n, ks).start()

    def routes(k, op):
        if k == 0:
            zk = z
        elif k == 1:
            zk = jnp.where(z == 1, 3, jnp.where(z == 3, 2, 1))
        else:
            zk = jnp.where(z == 0, 3, 0)
        for xp in range(NX):
            src = piece.at[k, xp]
            valid = jnp.where(gt == 1, xp <= x, xp >= x) if k == 0 else jnp.bool_(True)
            here = xp == x

            def send(device, p, n):
                c = remote(src, rall.at[p], rs.at[k, xp, n], rr.at[p], device)
                if op == "start":
                    c.start()
                else:
                    c.wait_send()

            def keep(p):
                if op == "start":
                    pltpu.make_async_copy(src, rall.at[p], rr.at[p]).start()

            @pl.when(jnp.logical_and(valid, jnp.logical_not(here)))
            def _():
                send(dev(z, xp, zl, y, core), zk * 4 + x, 0)

            if k == 0:
                @pl.when(valid)
                def _():
                    keep(z * 4 + xp)
            else:
                @pl.when(here)
                def _():
                    keep(zk * 4 + x)

                send(dev(zk, x, zl, y, core), z * 4 + xp, 1)

    lane = lax.broadcasted_iota(jnp.int32, (24, 128), 1)
    tall = lax.broadcasted_iota(jnp.int32, (VB, 128), 1)

    def final(k):
        v = [part[k, l, base + y * 2 + zl] + zbuf[k, l] for l in range(LT)]
        for xp in range(NX):
            turn = [v[l] if l == xp else pltpu.roll(v[l], (l - xp) % 4 * 32, 1) for l in range(LT)]
            w = jnp.where(tall < 32, turn[0], jnp.where(tall < 64, turn[1], turn[2]))

            @pl.when(gt == 1)
            def _():
                square[0:VB] = w

            @pl.when(gt == 0)
            def _():
                square[...] = jnp.concatenate([w, jnp.zeros((128 - VB, 128), F32)], axis=0).T

            r = [square[pl.ds(n, 24, stride=4), :] for n in range(4)]
            p = piece.at[k, xp]
            p[pl.ds(0, 24, stride=3), :] = jnp.where(lane < 96, r[0], pltpu.roll(r[1], 96, 1))
            p[pl.ds(1, 24, stride=3), :] = jnp.where(lane < 64, pltpu.roll(r[1], 96, 1), pltpu.roll(r[2], 64, 1))
            p[pl.ds(2, 24, stride=3), :] = jnp.where(lane < 32, pltpu.roll(r[2], 64, 1), pltpu.roll(r[3], 32, 1))
        routes(k, "start")

    def gather(j):
        for d in range(2):
            g_from(j, d).wait_recv()
            g_forward(j, d).start()
            if j < 2:
                g_chunk(j + 1, d).start()
        convert_g(xl, j)
        convert_g(xr, j)

    def behind(j):
        for d in range(2):
            g_behind(j, d).wait_recv()
        convert_g(x2, j)

    gather(0)
    pump(0)
    behind(0)
    stage1(0, 1)
    stage2(0, 1)
    core_copy(0, 1).start()
    pump(1)
    y_step1(0, 1)
    gather(1)
    y_step2(0, 1)
    behind(1)
    pump(2)
    stage1(1, 1)
    stage2(1, 1)
    core_copy(1, 1).start()
    y_step3(0, 1)

    def fetch(ks, m):
        for k in range(1, 1 + ks):
            if k == 1:
                p_wait(1, m)
            else:
                @pl.when(z == 2)
                def _():
                    p_wait(2, m)
            convert_s(k, m)

    def rest(ks):
        y_step1(1, 1)

        @pl.when(jnp.logical_not(ends))
        def _():
            gather(2)

        for m in range(3):
            fetch(ks, m)
        last = len(units) - 1
        for n in range(2, last + 1):
            if n == last:
                y_step1(n - 1, ks)
                y_step2(n - 2, ks)
            if units[n][0] == "rows":
                fetch(ks, units[n][1])
            stage1(n, ks)
            if 2 < n < last:
                y_step1(n - 1, ks)
                y_step2(n - 2, ks)
            stage2(n, ks)
            core_copy(n, ks).start()
            if n > 3:
                y_step3(n - 3, ks)
            if n == 2:
                @pl.when(ends)
                def _():
                    gather(2)
                pump(3)
            if n == 3:
                behind(2)
                pump(4)
            if n == 6:
                pump(5)
        y_step2(last - 1, ks)
        y_step1(last, ks)
        y_step3(last - 2, ks)
        for u in (0, 1, 4):
            z_copy(u, ks).wait_recv()
        final(0)
        y_step3(last - 1, ks)
        y_step2(last, ks)
        y_step3(last, ks)
        for n in range(2, last + 1):
            if n != 4:
                z_copy(n, ks).wait_recv()
        for k in range(1, 1 + ks):
            final(k)

    @pl.when(heavy)
    def _():
        rest(2)

    @pl.when(jnp.logical_not(heavy))
    def _():
        rest(1)

    for p in range(16):
        pltpu.make_async_copy(rall.at[p], rall.at[p], rr.at[p]).wait()
    for s in range(out.shape[0]):
        p = partners[0, s]
        out[s] = jnp.where(p >= 0, rall[jnp.maximum(p, 0)], 0.0)

    for j in range(LT):
        for d in range(2):
            g_chunk(j, d).wait_send()
            g_forward(j, d).wait_send()
    for c in t_sends:
        c.wait_send()

    @pl.when(ends)
    def _():
        for m in range(PN):
            p_relay(m).wait_send()

    def drain(n, ks):
        core_copy(n, ks).wait_send()
        for c in y_copies(n, ks):
            c.wait_send()
        z_copy(n, ks).wait_send()

    routes(0, "wait")
    routes(1, "wait")

    @pl.when(heavy)
    def _():
        for n in range(len(units)):
            drain(n, 2)
        routes(2, "wait")

    @pl.when(jnp.logical_not(heavy))
    def _():
        for n in range(len(units)):
            drain(n, 1)


def local(partners, cholesky, amplitudes):
    slots = partners.shape[1]
    chol = cholesky.reshape(VB, 2, CB, 2, 128).transpose(0, 1, 3, 2, 4)
    dma = pltpu.SemaphoreType.DMA
    res = pl.pallas_call(
        ladder,
        out_shape=jax.ShapeDtypeStruct((slots, 72, 128), F32),
        in_specs=[
            pl.BlockSpec(memory_space=pltpu.SMEM),
            pl.BlockSpec(memory_space=pl.ANY),
            pl.BlockSpec(memory_space=pltpu.VMEM),
        ],
        out_specs=pl.BlockSpec(memory_space=pltpu.VMEM),
        scratch_shapes=[
            pltpu.VMEM((NX, VB, 2, CB, 128), F32),
            pltpu.VMEM((3, VB, 2, CB, 128), F32),
            pltpu.VMEM((8, 128), F32),
            pltpu.VMEM((IJ, 8, 128), F32),
            pltpu.VMEM((256, 512), BF16),
            pltpu.VMEM((ROWS, 3 * QL), BF16),
            pltpu.VMEM((PN, 2 * PC * CB, 3 * QL), BF16),
            pltpu.VMEM((LT, CB * 128, 3 * QL), BF16),
            pltpu.VMEM((2, CB, ROWS, 128), BF16),
            pltpu.VMEM((3, LT, IJ, VB, 128), F32),
            pltpu.VMEM((3, LT, 8, VB, 128), F32),
            pltpu.VMEM((6, 3, LT, VB, 128), F32),
            pltpu.VMEM((3, LT, VB, 128), F32),
            pltpu.VMEM((128, 128), F32),
            pltpu.VMEM((3, NX, 72, 128), F32),
            pltpu.VMEM((16, 72, 128), F32),
            dma((2,)),
            dma((3, 4)), dma((3, 4)),
            dma((3, PN)), dma((3, PN)),
            dma((15,)), dma((16,)),
            dma((9,)), dma((9,)),
            dma((9, 6)), dma((9, 6)),
            dma((9,)), dma((9,)),
            dma((3, NX, 2)), dma((16,)),
        ],
        compiler_params=pltpu.CompilerParams(
            collective_id=0, has_side_effects=True, vmem_limit_bytes=56 * 1024 * 1024
        ),
    )(partners, chol, amplitudes)
    return res.reshape(slots, 1, VB * VB)


def solution(mesh):
    return jax.shard_map(
        local,
        mesh=mesh,
        in_specs=(P("ab", None), P("ab", None, "ij"), P("ij", None)),
        out_specs=P("ab", "ij", None),
        check_vma=False,
    )
```

```python
import jax
import jax.numpy as jnp
from jax import lax
from jax.experimental import pallas as pl
from jax.experimental.pallas import tpu as pltpu
from jax.sharding import PartitionSpec as P

MESH = pl.DeviceIdType.MESH
F32 = jnp.float32
BF16 = jnp.bfloat16
VB = 96
CB = 8
QL = 256
ROWS = VB * CB
NX = 4
LT = 3
CH = 32
PC = 16
PN = 6
IJ = 16


def split(v):
    hi = v.astype(BF16)
    lo = (v - hi.astype(F32)).astype(BF16)
    return hi, lo


def ladder(
    partners, chol, amp, out,
    gbuf, sbuf, abuf, tbuf, wide, left, leftp, right, tile, part, cbuf, ybuf, zbuf, square, piece, rall,
    lsem, gs, gr, ps, pr, ts, tr, cs, cr, ys, yr, zs, zr, rs, rr,
):
    ab = lax.axis_index("ab")
    ij = lax.axis_index("ij")
    z, x = lax.div(ab, 4), lax.rem(ab, 4)
    zl, y, core = lax.div(ij, 8), lax.rem(lax.div(ij, 2), 4), lax.rem(ij, 2)

    def dev(z_, x_, zl_, y_, core_):
        return (z_ * 4 + x_, zl_ * 8 + y_ * 2 + core_)

    def mod4(v):
        return lax.rem(v + 8, 4)

    gt = jnp.where(z < 2, 1, 0)
    xl, xr, x2 = mod4(x - 1), mod4(x + 1), mod4(x + 2)
    yl, yr_, y2 = mod4(y - 1), mod4(y + 1), mod4(y + 2)
    heavy = lax.rem(z, 2) == 0
    ends = jnp.logical_or(z == 0, z == 3)

    barrier = pltpu.get_barrier_semaphore()
    peers = [dev(z, x, zl, y, 1 - core), dev(z, x, 1 - zl, y, core)]
    for n in range(1, 4):
        peers.append(dev(z, x, zl, mod4(y + n), core))
        peers.append(dev(z, mod4(x + n), zl, y, core))
        peers.append(dev(mod4(z + n), x, zl, y, core))
    for peer in peers:
        pl.semaphore_signal(barrier, inc=1, device_id=peer, device_id_type=MESH)
    own_g = chol.at[:, gt]
    local_g = pltpu.make_async_copy(own_g, gbuf.at[x], lsem.at[0])
    local_s = pltpu.make_async_copy(chol.at[:, 1 - gt], sbuf.at[0], lsem.at[1])
    local_g.start()
    local_s.start()
    row = jnp.concatenate([amp[...], jnp.zeros((1, 64), F32)], axis=1)
    abuf[...] = jnp.broadcast_to(row, (8, 128))
    pl.semaphore_wait(barrier, len(peers))

    def remote(src, dst, send, recv, device):
        return pltpu.make_async_remote_copy(
            src_ref=src, dst_ref=dst, send_sem=send, recv_sem=recv, device_id=device, device_id_type=MESH
        )

    to_right, to_left = dev(z, xr, zl, y, core), dev(z, xl, zl, y, core)

    def g_chunk(j, d):
        return remote(
            chol.at[pl.ds(j * CH, CH), gt], gbuf.at[x, pl.ds(j * CH, CH)], gs.at[j, d], gr.at[j, d],
            (to_right, to_left)[d],
        )

    def g_from(j, d):
        at = gbuf.at[(xl, xr)[d], pl.ds(j * CH, CH)]
        return remote(at, at, gs.at[j, d], gr.at[j, d], (to_right, to_left)[d])

    def g_forward(j, d):
        at = gbuf.at[(xl, xr)[d], pl.ds(j * CH + d * 16, 16)]
        return remote(at, at, gs.at[j, 2 + d], gr.at[j, 2 + d], (to_right, to_left)[d])

    def g_behind(j, d):
        at = gbuf.at[x2, pl.ds(j * CH + d * 16, 16)]
        return remote(at, at, gs.at[j, 2 + d], gr.at[j, 2 + d], (to_right, to_left)[d])

    def p_send(m):
        rows = pl.ds(m * PC, PC)
        to = jnp.where(ends, 2, 1)
        return remote(
            chol.at[rows, 1 - lax.rem(z, 2)], sbuf.at[to, rows], ps.at[0, m], pr.at[to, m],
            dev(3 * (1 - lax.rem(z, 2)), x, zl, y, core),
        )

    def p_send_up(m):
        rows = pl.ds(m * PC, PC)
        return remote(
            chol.at[rows, 1], sbuf.at[1, rows], ps.at[1, m], pr.at[1, m], dev(2, x, zl, y, core)
        )

    def p_relay(m):
        rows = pl.ds(m * PC, PC)
        to = jnp.where(z == 0, 1, 2)
        return remote(
            sbuf.at[2, rows], sbuf.at[to, rows], ps.at[2, m], pr.at[to, m], dev(to, x, zl, y, core)
        )

    def p_wait(k, m):
        at = sbuf.at[k, pl.ds(m * PC, PC)]
        remote(at, at, ps.at[0, m], pr.at[k, m], to_right).wait_recv()

    for d in range(2):
        g_chunk(0, d).start()
    def p_start(m):
        p_send(m).start()

        @pl.when(z == 1)
        def _():
            p_send_up(m).start()

    def pump(m):
        p_send(m).wait_send()

        @pl.when(z == 1)
        def _():
            p_send_up(m).wait_send()

        if m + 2 < PN:
            p_start(m + 2)

        @pl.when(ends)
        def _():
            p_wait(2, m)
            p_relay(m).start()

    p_start(0)
    p_start(1)
    def t_copy(n, send):
        if n == 0:
            at, device = tbuf.at[core if send else 1 - core, y, zl], dev(z, x, zl, y, 1 - core)
        elif n == 1:
            at, device = tbuf.at[:, y, zl if send else 1 - zl], dev(z, x, 1 - zl, y, core)
        else:
            at, device = tbuf.at[:, y if send else mod4(y - n + 1)], dev(z, x, zl, mod4(y + n - 1), core)
        return remote(at, at, ts.at[n], tr.at[n], device)

    tbuf[core, y, zl] = abuf[...]
    t_copy(0, True).start()

    gview = gbuf.reshape(NX, VB * 2 * CB, 128)

    def convert_g(n, j):
        for e in range(CB):
            v = jnp.concatenate(
                [gview[n, pl.ds(j * CH * 16 + h * CB + e, CH, stride=2 * CB), :] for h in range(2)], axis=1
            )
            hi, lo = split(v)
            at = pl.ds(pl.multiple_of(e * 128 + n * CH, CH), CH)
            right[j, at, 0:QL] = hi
            right[j, at, QL:2 * QL] = lo
            right[j, at, 2 * QL:3 * QL] = hi

    def convert_s(k, m):
        for h in range(2):
            v = sbuf[k, pl.ds(m * PC, PC), h].reshape(PC * CB, 128)
            hi, lo = split(v)
            to = left.at[pl.ds(m * PC * CB, PC * CB)] if k == 0 else leftp.at[m, pl.ds((k - 1) * PC * CB, PC * CB)]
            to[:, h * 128:h * 128 + 128] = hi
            to[:, QL + h * 128:QL + h * 128 + 128] = hi
            to[:, 2 * QL + h * 128:2 * QL + h * 128 + 128] = lo

    local_g.wait()
    local_s.wait()
    for j in range(LT):
        convert_g(x, j)
    for m in range(PN):
        convert_s(0, m)

    for n in range(2):
        t_copy(n, False).wait_recv()
        for o in ((1,), (2, 3, 4))[n]:
            t_copy(o, True).start()
    for n in range(2, 5):
        t_copy(n, False).wait_recv()
    source = lax.broadcasted_iota(jnp.int32, (128, 512), 0)
    target = lax.broadcasted_iota(jnp.int32, (128, 512), 1)
    outer, inner = lax.div(target, 64), lax.rem(target, 8)
    pick = jnp.where(source == jnp.where(gt == 1, inner * 8 + outer, outer * 8 + inner), 1.0, 0.0).astype(BF16)
    same = lax.rem(source, 8) == lax.rem(lax.div(target, 8), 8)
    for n, v in enumerate(split(tbuf.reshape(IJ, 8, 128)[:, 0, :])):
        w = jnp.dot(v, pick, preferred_element_type=F32)
        w = jnp.broadcast_to(w[:, None, :], (IJ, 8, 512)).reshape(128, 512)
        wide[n * 128:(n + 1) * 128] = jnp.where(same, w, 0.0).astype(BF16)

    units = [("own", 0), ("own", 1), ("half", 0), ("half", 1), ("own", 2), ("half", 2)]
    units += [("rows", m) for m in range(3, PN)]

    def stage1(n, ks):
        kind, v = units[n]
        size = 256 if kind == "own" else 128 * ks

        def column(en, carry):
            at = pl.ds(en * 256, 256) if isinstance(en, int) else pl.ds(pl.multiple_of(en * 256, 256), 256)
            for r in range(3):
                if kind == "own":
                    lhs = left[r * 256:(r + 1) * 256, :]
                else:
                    lhs = leftp[r if kind == "half" else v, 0:size, :]
                t = lax.dot_general(
                    lhs, right[r if kind == "rows" else v, at, :],
                    (((1,), (1,)), ((), ())), preferred_element_type=F32,
                )
                hi, lo = split(t)
                for u in range(256 // 128):
                    tile[0, en * 2 + u, r * size:(r + 1) * size, :] = hi[:, u * 128:(u + 1) * 128]
                    tile[1, en * 2 + u, r * size:(r + 1) * size, :] = lo[:, u * 128:(u + 1) * 128]
            return carry

        for en in range(CB * 128 // 256):
            column(en, 0)

    def stage2(n, ks):
        kind, w = units[n]

        many = 4 if kind == "own" else 2 * ks

        def rows(it, carry):
            cols = []
            for h in range(2):
                at = [(it * many + u) * 64 for u in range(many)]
                cols.append(
                    jnp.concatenate(
                        [jnp.concatenate([tile[h, e, pl.ds(b, 64), :] for e in range(CB)], axis=0) for b in at], axis=1
                    )
                )
            r = jnp.dot(wide[...], cols[0], preferred_element_type=F32)
            q = jnp.dot(wide[0:128], cols[1], preferred_element_type=F32)
            r = r[:128] + r[128:] + q
            for u in range(many):
                v = r[:, u * 128:(u + 1) * 128].reshape(IJ, 8, 128)
                if kind == "own":
                    part[0, w, :, pl.ds((it * many + u) * 8, 8), :] = v
                elif kind == "half":
                    part[1 + u // 2, w, :, pl.ds(it * PC + u % 2 * 8, 8), :] = v
                else:
                    part[1 + u // 2, it, :, pl.ds(w * PC + u % 2 * 8, 8), :] = v
            return carry

        for it in range(3):
            rows(it, 0)

    base, away = core * 8, (1 - core) * 8
    sibling = dev(z, x, zl, y, 1 - core)
    y_left, y_right = dev(z, x, zl, yl, core), dev(z, x, zl, yr_, core)
    z_other = dev(z, x, 1 - zl, y, core)

    def reach(n):
        kind, v = units[n]
        return {"own": (v, 1, 0, VB), "half": (v, 1, 0, 3 * PC), "rows": (0, LT, v * PC, PC)}[kind]

    def spans(n, ks):
        l, ln, a, an = reach(n)
        return pl.ds(0, 1) if units[n][0] == "own" else pl.ds(1, ks), pl.ds(l, ln), pl.ds(a, an)

    def blocks(n, ks):
        l, ln, a, an = reach(n)
        ks_ = [0] if units[n][0] == "own" else range(1, 1 + ks)
        return [(k, l_) for k in ks_ for l_ in range(l, l + ln)], slice(a, a + an)

    def core_copy(n, ks):
        k, l, a = spans(n, ks)
        return remote(
            part.at[k, l, pl.ds(away, 8), a], cbuf.at[k, l, pl.ds(0, 8), a], cs.at[n], cr.at[n], sibling
        )

    def y_copies(n, ks):
        k, l, a = spans(n, ks)

        def one(c, y_, o, device):
            return remote(
                part.at[k, l, base + y_ * 2 + o, a], ybuf.at[c, k, l, a], ys.at[n, c], yr.at[n, c], device
            )

        return [
            one(0, y2, 0, y_right), one(1, yr_, 1, y_right), one(2, y2, 1, y_left),
            one(3, yl, 0, y_left), one(4, yr_, 0, y_right), one(5, yl, 1, y_left),
        ]

    def z_copy(n, ks):
        k, l, a = spans(n, ks)
        return remote(
            part.at[k, l, base + y * 2 + (1 - zl), a], zbuf.at[k, l, a], zs.at[n], zr.at[n], z_other
        )

    def y_step1(n, ks):
        core_copy(n, ks).wait_recv()
        kls, a = blocks(n, ks)

        def add(i, carry):
            for k, l in kls:
                part[k, l, base + i, a, :] = part[k, l, base + i, a, :] + cbuf[k, l, i, a, :]
            return carry

        lax.fori_loop(0, 8, add, 0)
        for c in y_copies(n, ks)[:4]:
            c.start()

    def y_step2(n, ks):
        copies = y_copies(n, ks)
        kls, a = blocks(n, ks)
        for first, i, then in ((0, base + yr_ * 2, 4), (2, base + yl * 2 + 1, 5)):
            copies[first].wait_recv()
            for k, l in kls:
                part[k, l, i, a, :] = part[k, l, i, a, :] + ybuf[first, k, l, a, :]
            copies[then].start()

    def y_step3(n, ks):
        copies = y_copies(n, ks)
        kls, a = blocks(n, ks)
        for o, pair in enumerate(((3, 4), (1, 5))):
            for c in pair:
                copies[c].wait_recv()
            i = base + y * 2 + o
            for k, l in kls:
                part[k, l, i, a, :] = part[k, l, i, a, :] + ybuf[pair[0], k, l, a, :] + ybuf[pair[1], k, l, a, :]
        z_copy(n, ks).start()

    def routes(k, h, op):
        if k == 0:
            zk = z
        elif k == 1:
            zk = jnp.where(z == 1, 3, jnp.where(z == 3, 2, 1))
        else:
            zk = jnp.where(z == 0, 3, 0)
        for xp in range(NX):
            src = piece.at[k, xp, h]
            valid = jnp.where(gt == 1, xp <= x, xp >= x) if k == 0 else jnp.bool_(True)
            here = xp == x

            def send(device, p, n):
                c = remote(src, rall.at[p, h], rs.at[k, xp, h, n], rr.at[p, h], device)
                if op == "start":
                    c.start()
                else:
                    c.wait_send()

            def keep(p):
                if op == "start":
                    pltpu.make_async_copy(src, rall.at[p, h], rr.at[p, h]).start()

            @pl.when(jnp.logical_and(valid, jnp.logical_not(here)))
            def _():
                send(dev(z, xp, zl, y, core), zk * 4 + x, 0)

            if k == 0:
                @pl.when(valid)
                def _():
                    keep(z * 4 + xp)
            else:
                @pl.when(here)
                def _():
                    keep(zk * 4 + x)

                send(dev(zk, x, zl, y, core), z * 4 + xp, 1)

    lane = lax.broadcasted_iota(jnp.int32, (12, 128), 1)

    def pack(k, xp, h, first):
        r = [square[pl.ds(first + n, 12, stride=4), :] for n in range(4)]
        p = piece.at[k, xp, h]
        p[pl.ds(0, 12, stride=3), :] = jnp.where(lane < 96, r[0], pltpu.roll(r[1], 96, 1))
        p[pl.ds(1, 12, stride=3), :] = jnp.where(lane < 64, pltpu.roll(r[1], 96, 1), pltpu.roll(r[2], 64, 1))
        p[pl.ds(2, 12, stride=3), :] = jnp.where(lane < 32, pltpu.roll(r[2], 64, 1), pltpu.roll(r[3], 32, 1))

    def block(k, xp, a, an):
        v = [part[k, l, base + y * 2 + zl, a:a + an] + zbuf[k, l, a:a + an] for l in range(LT)]
        turn = [v[l] if l == xp else pltpu.roll(v[l], (l - xp) % 4 * 32, 1) for l in range(LT)]
        tall = lax.broadcasted_iota(jnp.int32, (an, 128), 1)
        return jnp.where(tall < 32, turn[0], jnp.where(tall < 64, turn[1], turn[2]))

    def final_half(k, h):
        for xp in range(NX):
            square[0:48] = block(k, xp, h * 48, 48)
            pack(k, xp, h, 0)
        routes(k, h, "start")

    def final_turned(k):
        for xp in range(NX):
            w = block(k, xp, 0, VB)
            square[...] = jnp.concatenate([w, jnp.zeros((128 - VB, 128), F32)], axis=0).T
            for h in range(2):
                pack(k, xp, h, h * 48)
        for h in range(2):
            routes(k, h, "start")

    def final(k, hs):
        @pl.when(gt == 1)
        def _():
            for h in hs:
                final_half(k, h)

        if 1 in hs:
            @pl.when(gt == 0)
            def _():
                final_turned(k)

    def gather(j):
        for d in range(2):
            g_from(j, d).wait_recv()
            g_forward(j, d).start()
            if j < 2:
                g_chunk(j + 1, d).start()
        convert_g(xl, j)
        convert_g(xr, j)

    def behind(j):
        for d in range(2):
            g_behind(j, d).wait_recv()
        convert_g(x2, j)

    gather(0)
    pump(0)
    behind(0)
    stage1(0, 1)
    stage2(0, 1)
    core_copy(0, 1).start()
    pump(1)
    y_step1(0, 1)
    gather(1)
    y_step2(0, 1)
    behind(1)
    pump(2)
    stage1(1, 1)
    stage2(1, 1)
    core_copy(1, 1).start()
    y_step3(0, 1)

    def fetch(ks, m):
        for k in range(1, 1 + ks):
            if k == 1:
                p_wait(1, m)
            else:
                @pl.when(z == 2)
                def _():
                    p_wait(2, m)
            convert_s(k, m)

    def rest(ks):
        y_step1(1, 1)

        @pl.when(jnp.logical_not(ends))
        def _():
            gather(2)

        for m in range(3):
            fetch(ks, m)
        last = len(units) - 1
        for n in range(2, last + 1):
            if n == last:
                y_step1(n - 1, ks)
                y_step2(n - 2, ks)
            if units[n][0] == "rows":
                fetch(ks, units[n][1])
            stage1(n, ks)
            if 2 < n < last:
                if n == 4:
                    @pl.when(jnp.logical_not(ends))
                    def _():
                        y_step1(3, ks)
                else:
                    y_step1(n - 1, ks)
                y_step2(n - 2, ks)
            stage2(n, ks)
            core_copy(n, ks).start()
            if n > 3:
                y_step3(n - 3, ks)
            if n == 3:
                @pl.when(ends)
                def _():
                    y_step1(3, ks)
                    gather(2)

                pump(3)
                behind(2)
            if n == 4:
                pump(4)
            if n == 6:
                pump(5)
        y_step2(last - 1, ks)
        y_step1(last, ks)
        for u in (0, 1, 4):
            z_copy(u, ks).wait_recv()
        final(0, (0, 1))
        y_step3(last - 2, ks)
        for u in (2, 3, 5):
            z_copy(u, ks).wait_recv()
        for k in range(ks, 0, -1):
            final(k, (0,))
        y_step3(last - 1, ks)
        y_step2(last, ks)
        y_step3(last, ks)
        for u in (6, 7, 8):
            z_copy(u, ks).wait_recv()
        for k in range(ks, 0, -1):
            final(k, (1,))

    @pl.when(heavy)
    def _():
        rest(2)

    @pl.when(jnp.logical_not(heavy))
    def _():
        rest(1)

    for p in range(16):
        for h in range(2):
            pltpu.make_async_copy(rall.at[p, h], rall.at[p, h], rr.at[p, h]).wait()
    for s in range(out.shape[0]):
        p = partners[0, s]
        for h in range(2):
            out[s, h * 36:h * 36 + 36] = jnp.where(p >= 0, rall[jnp.maximum(p, 0), h, 0:36], 0.0)

    for j in range(LT):
        for d in range(2):
            g_chunk(j, d).wait_send()
            g_forward(j, d).wait_send()
    for n in range(5):
        t_copy(n, True).wait_send()

    @pl.when(ends)
    def _():
        for m in range(PN):
            p_relay(m).wait_send()

    def drain(n, ks):
        core_copy(n, ks).wait_send()
        for c in y_copies(n, ks):
            c.wait_send()
        z_copy(n, ks).wait_send()

    def drain_routes(k):
        for h in range(2):
            routes(k, h, "wait")

    drain_routes(0)
    drain_routes(1)

    @pl.when(heavy)
    def _():
        for n in range(len(units)):
            drain(n, 2)
        drain_routes(2)

    @pl.when(jnp.logical_not(heavy))
    def _():
        for n in range(len(units)):
            drain(n, 1)


def local(partners, cholesky, amplitudes):
    slots = partners.shape[1]
    chol = cholesky.reshape(VB, 2, CB, 2, 128).transpose(0, 1, 3, 2, 4)
    dma = pltpu.SemaphoreType.DMA
    res = pl.pallas_call(
        ladder,
        out_shape=jax.ShapeDtypeStruct((slots, 72, 128), F32),
        in_specs=[
            pl.BlockSpec(memory_space=pltpu.SMEM),
            pl.BlockSpec(memory_space=pl.ANY),
            pl.BlockSpec(memory_space=pltpu.VMEM),
        ],
        out_specs=pl.BlockSpec(memory_space=pltpu.VMEM),
        scratch_shapes=[
            pltpu.VMEM((NX, VB, 2, CB, 128), F32),
            pltpu.VMEM((3, VB, 2, CB, 128), F32),
            pltpu.VMEM((8, 128), F32),
            pltpu.VMEM((2, 4, 2, 8, 128), F32),
            pltpu.VMEM((256, 512), BF16),
            pltpu.VMEM((ROWS, 3 * QL), BF16),
            pltpu.VMEM((PN, 2 * PC * CB, 3 * QL), BF16),
            pltpu.VMEM((LT, CB * 128, 3 * QL), BF16),
            pltpu.VMEM((2, CB, ROWS, 128), BF16),
            pltpu.VMEM((3, LT, IJ, VB, 128), F32),
            pltpu.VMEM((3, LT, 8, VB, 128), F32),
            pltpu.VMEM((6, 3, LT, VB, 128), F32),
            pltpu.VMEM((3, LT, VB, 128), F32),
            pltpu.VMEM((128, 128), F32),
            pltpu.VMEM((3, NX, 2, 40, 128), F32),
            pltpu.VMEM((16, 2, 40, 128), F32),
            dma((2,)),
            dma((3, 4)), dma((3, 4)),
            dma((3, PN)), dma((3, PN)),
            dma((5,)), dma((5,)),
            dma((9,)), dma((9,)),
            dma((9, 6)), dma((9, 6)),
            dma((9,)), dma((9,)),
            dma((3, NX, 2, 2)), dma((16, 2)),
        ],
        compiler_params=pltpu.CompilerParams(
            collective_id=0, has_side_effects=True, vmem_limit_bytes=56 * 1024 * 1024
        ),
    )(partners, chol, amplitudes)
    return res.reshape(slots, 1, VB * VB)


def solution(mesh):
    return jax.shard_map(
        local,
        mesh=mesh,
        in_specs=(P("ab", None), P("ab", None, "ij"), P("ij", None)),
        out_specs=P("ab", "ij", None),
        check_vma=False,
    )
```

```python
import jax
import jax.numpy as jnp
from jax import lax
from jax.experimental import pallas as pl
from jax.experimental.pallas import tpu as pltpu
from jax.sharding import PartitionSpec as P

MESH = pl.DeviceIdType.MESH
F32 = jnp.float32
BF16 = jnp.bfloat16
VB = 96
CB = 8
QL = 256
ROWS = VB * CB
NX = 4
LT = 3
CH = 32
PC = 16
PN = 6
IJ = 16


def split(v):
    hi = v.astype(BF16)
    lo = (v - hi.astype(F32)).astype(BF16)
    return hi, lo


def ladder(
    partners, chol, amp, out,
    gbuf, sbuf, abuf, tbuf, wide, left, leftp, right, tile, part, cbuf, ybuf, zbuf, square, piece, rall,
    lsem, gs, gr, ps, pr, ts, tr, cs, cr, ys, yr, zs, zr, rs, rr,
):
    ab = lax.axis_index("ab")
    ij = lax.axis_index("ij")
    z, x = lax.div(ab, 4), lax.rem(ab, 4)
    zl, y, core = lax.div(ij, 8), lax.rem(lax.div(ij, 2), 4), lax.rem(ij, 2)

    def dev(z_, x_, zl_, y_, core_):
        return (z_ * 4 + x_, zl_ * 8 + y_ * 2 + core_)

    def mod4(v):
        return lax.rem(v + 8, 4)

    gt = jnp.where(z < 2, 1, 0)
    xl, xr, x2 = mod4(x - 1), mod4(x + 1), mod4(x + 2)
    yl, yr_, y2 = mod4(y - 1), mod4(y + 1), mod4(y + 2)
    heavy = lax.rem(z, 2) == 0
    ends = jnp.logical_or(z == 0, z == 3)

    barrier = pltpu.get_barrier_semaphore()
    peers = [dev(z, x, zl, y, 1 - core), dev(z, x, 1 - zl, y, core)]
    for n in range(1, 4):
        peers.append(dev(z, x, zl, mod4(y + n), core))
        peers.append(dev(z, mod4(x + n), zl, y, core))
        peers.append(dev(mod4(z + n), x, zl, y, core))
    for peer in peers:
        pl.semaphore_signal(barrier, inc=1, device_id=peer, device_id_type=MESH)
    own_g = chol.at[:, gt]
    local_g = pltpu.make_async_copy(own_g, gbuf.at[x], lsem.at[0])
    local_s = pltpu.make_async_copy(chol.at[:, 1 - gt], sbuf.at[0], lsem.at[1])
    local_g.start()
    local_s.start()
    row = jnp.concatenate([amp[...], jnp.zeros((1, 64), F32)], axis=1)
    abuf[...] = jnp.broadcast_to(row, (8, 128))
    pl.semaphore_wait(barrier, len(peers))

    def remote(src, dst, send, recv, device):
        return pltpu.make_async_remote_copy(
            src_ref=src, dst_ref=dst, send_sem=send, recv_sem=recv, device_id=device, device_id_type=MESH
        )

    to_right, to_left = dev(z, xr, zl, y, core), dev(z, xl, zl, y, core)

    def g_chunk(j, d):
        return remote(
            chol.at[pl.ds(j * CH, CH), gt], gbuf.at[x, pl.ds(j * CH, CH)], gs.at[j, d], gr.at[j, d],
            (to_right, to_left)[d],
        )

    def g_from(j, d):
        at = gbuf.at[(xl, xr)[d], pl.ds(j * CH, CH)]
        return remote(at, at, gs.at[j, d], gr.at[j, d], (to_right, to_left)[d])

    def g_forward(j, d):
        at = gbuf.at[(xl, xr)[d], pl.ds(j * CH + d * 16, 16)]
        return remote(at, at, gs.at[j, 2 + d], gr.at[j, 2 + d], (to_right, to_left)[d])

    def g_behind(j, d):
        at = gbuf.at[x2, pl.ds(j * CH + d * 16, 16)]
        return remote(at, at, gs.at[j, 2 + d], gr.at[j, 2 + d], (to_right, to_left)[d])

    def p_send(m):
        rows = pl.ds(m * PC, PC)
        to = jnp.where(ends, 2, 1)
        return remote(
            chol.at[rows, 1 - lax.rem(z, 2)], sbuf.at[to, rows], ps.at[0, m], pr.at[to, m],
            dev(3 * (1 - lax.rem(z, 2)), x, zl, y, core),
        )

    def p_send_up(m):
        rows = pl.ds(m * PC, PC)
        return remote(
            chol.at[rows, 1], sbuf.at[1, rows], ps.at[1, m], pr.at[1, m], dev(2, x, zl, y, core)
        )

    def p_relay(m):
        rows = pl.ds(m * PC, PC)
        to = jnp.where(z == 0, 1, 2)
        return remote(
            sbuf.at[2, rows], sbuf.at[to, rows], ps.at[2, m], pr.at[to, m], dev(to, x, zl, y, core)
        )

    def p_wait(k, m):
        at = sbuf.at[k, pl.ds(m * PC, PC)]
        remote(at, at, ps.at[0, m], pr.at[k, m], to_right).wait_recv()

    for d in range(2):
        g_chunk(0, d).start()
    def p_start(m):
        p_send(m).start()

        @pl.when(z == 1)
        def _():
            p_send_up(m).start()

    def pump(m):
        p_send(m).wait_send()

        @pl.when(z == 1)
        def _():
            p_send_up(m).wait_send()

        if m + 2 < PN:
            p_start(m + 2)

        @pl.when(ends)
        def _():
            p_wait(2, m)
            p_relay(m).start()

    p_start(0)
    p_start(1)
    def t_copy(n, send):
        if n == 0:
            at, device = tbuf.at[core if send else 1 - core, y, zl], dev(z, x, zl, y, 1 - core)
        elif n == 1:
            at, device = tbuf.at[:, y, zl if send else 1 - zl], dev(z, x, 1 - zl, y, core)
        else:
            at, device = tbuf.at[:, y if send else mod4(y - n + 1)], dev(z, x, zl, mod4(y + n - 1), core)
        return remote(at, at, ts.at[n], tr.at[n], device)

    tbuf[core, y, zl] = abuf[...]
    t_copy(0, True).start()

    gview = gbuf.reshape(NX, VB * 2 * CB, 128)

    def convert_g(n, j):
        for e in range(CB):
            v = jnp.concatenate(
                [gview[n, pl.ds(j * CH * 16 + h * CB + e, CH, stride=2 * CB), :] for h in range(2)], axis=1
            )
            hi, lo = split(v)
            at = pl.ds(pl.multiple_of(e * 128 + n * CH, CH), CH)
            right[j, at, 0:QL] = hi
            right[j, at, QL:2 * QL] = lo
            right[j, at, 2 * QL:3 * QL] = hi

    def convert_s(k, m):
        for h in range(2):
            v = sbuf[k, pl.ds(m * PC, PC), h].reshape(PC * CB, 128)
            hi, lo = split(v)
            to = left.at[pl.ds(m * PC * CB, PC * CB)] if k == 0 else leftp.at[m, pl.ds((k - 1) * PC * CB, PC * CB)]
            to[:, h * 128:h * 128 + 128] = hi
            to[:, QL + h * 128:QL + h * 128 + 128] = hi
            to[:, 2 * QL + h * 128:2 * QL + h * 128 + 128] = lo

    local_g.wait()
    local_s.wait()
    for j in range(LT):
        convert_g(x, j)
    for m in range(PN):
        convert_s(0, m)

    for n in range(2):
        t_copy(n, False).wait_recv()
        for o in ((1,), (2, 3, 4))[n]:
            t_copy(o, True).start()
    for n in range(2, 5):
        t_copy(n, False).wait_recv()
    source = lax.broadcasted_iota(jnp.int32, (128, 512), 0)
    target = lax.broadcasted_iota(jnp.int32, (128, 512), 1)
    outer, inner = lax.div(target, 64), lax.rem(target, 8)
    pick = jnp.where(source == jnp.where(gt == 1, inner * 8 + outer, outer * 8 + inner), 1.0, 0.0).astype(BF16)
    same = lax.rem(source, 8) == lax.rem(lax.div(target, 8), 8)
    for n, v in enumerate(split(tbuf.reshape(IJ, 8, 128)[:, 0, :])):
        w = jnp.dot(v, pick, preferred_element_type=F32)
        w = jnp.broadcast_to(w[:, None, :], (IJ, 8, 512)).reshape(128, 512)
        wide[n * 128:(n + 1) * 128] = jnp.where(same, w, 0.0).astype(BF16)

    units = [("own", 0), ("own", 1), ("half", 0), ("half", 1), ("own", 2), ("half", 2)]
    units += [("rows", m) for m in range(3, PN)]

    def stage1(n, ks):
        kind, v = units[n]
        size = 256 if kind == "own" else 128 * ks

        def column(en, carry):
            at = pl.ds(en * 256, 256) if isinstance(en, int) else pl.ds(pl.multiple_of(en * 256, 256), 256)
            for r in range(3):
                if kind == "own":
                    lhs = left[r * 256:(r + 1) * 256, :]
                else:
                    lhs = leftp[r if kind == "half" else v, 0:size, :]
                t = lax.dot_general(
                    lhs, right[r if kind == "rows" else v, at, :],
                    (((1,), (1,)), ((), ())), preferred_element_type=F32,
                )
                hi, lo = split(t)
                for u in range(256 // 128):
                    tile[0, en * 2 + u, r * size:(r + 1) * size, :] = hi[:, u * 128:(u + 1) * 128]
                    tile[1, en * 2 + u, r * size:(r + 1) * size, :] = lo[:, u * 128:(u + 1) * 128]
            return carry

        for en in range(CB * 128 // 256):
            column(en, 0)

    def stage2(n, ks):
        kind, w = units[n]

        many = 4 if kind == "own" else 2 * ks

        def rows(it, carry):
            cols = []
            for h in range(2):
                at = [(it * many + u) * 64 for u in range(many)]
                cols.append(
                    jnp.concatenate(
                        [jnp.concatenate([tile[h, e, pl.ds(b, 64), :] for e in range(CB)], axis=0) for b in at], axis=1
                    )
                )
            r = jnp.dot(wide[...], cols[0], preferred_element_type=F32)
            q = jnp.dot(wide[0:128], cols[1], preferred_element_type=F32)
            r = r[:128] + r[128:] + q
            for u in range(many):
                v = r[:, u * 128:(u + 1) * 128].reshape(IJ, 8, 128)
                if kind == "own":
                    part[0, w, :, pl.ds((it * many + u) * 8, 8), :] = v
                elif kind == "half":
                    part[1 + u // 2, w, :, pl.ds(it * PC + u % 2 * 8, 8), :] = v
                else:
                    part[1 + u // 2, it, :, pl.ds(w * PC + u % 2 * 8, 8), :] = v
            return carry

        for it in range(3):
            rows(it, 0)

    base, away = core * 8, (1 - core) * 8
    sibling = dev(z, x, zl, y, 1 - core)
    y_left, y_right = dev(z, x, zl, yl, core), dev(z, x, zl, yr_, core)
    z_other = dev(z, x, 1 - zl, y, core)

    def reach(n):
        kind, v = units[n]
        return {"own": (v, 1, 0, VB), "half": (v, 1, 0, 3 * PC), "rows": (0, LT, v * PC, PC)}[kind]

    def spans(n, ks):
        l, ln, a, an = reach(n)
        return pl.ds(0, 1) if units[n][0] == "own" else pl.ds(1, ks), pl.ds(l, ln), pl.ds(a, an)

    def blocks(n, ks):
        l, ln, a, an = reach(n)
        ks_ = [0] if units[n][0] == "own" else range(1, 1 + ks)
        return [(k, l_) for k in ks_ for l_ in range(l, l + ln)], slice(a, a + an)

    def core_copy(n, ks):
        k, l, a = spans(n, ks)
        return remote(
            part.at[k, l, pl.ds(away, 8), a], cbuf.at[k, l, pl.ds(0, 8), a], cs.at[n], cr.at[n], sibling
        )

    def y_copies(n, ks):
        k, l, a = spans(n, ks)

        def one(c, y_, o, device):
            return remote(
                part.at[k, l, base + y_ * 2 + o, a], ybuf.at[c, k, l, a], ys.at[n, c], yr.at[n, c], device
            )

        return [
            one(0, y2, 0, y_right), one(1, yr_, 1, y_right), one(2, y2, 1, y_left),
            one(3, yl, 0, y_left), one(4, yr_, 0, y_right), one(5, yl, 1, y_left),
        ]

    def z_copy(n, ks):
        k, l, a = spans(n, ks)
        return remote(
            part.at[k, l, base + y * 2 + (1 - zl), a], zbuf.at[k, l, a], zs.at[n], zr.at[n], z_other
        )

    def y_step1(n, ks):
        core_copy(n, ks).wait_recv()
        kls, a = blocks(n, ks)

        def add(i, carry):
            for k, l in kls:
                part[k, l, base + i, a, :] = part[k, l, base + i, a, :] + cbuf[k, l, i, a, :]
            return carry

        lax.fori_loop(0, 8, add, 0)
        for c in y_copies(n, ks)[:4]:
            c.start()

    def y_step2(n, ks):
        copies = y_copies(n, ks)
        kls, a = blocks(n, ks)
        for first, i, then in ((0, base + yr_ * 2, 4), (2, base + yl * 2 + 1, 5)):
            copies[first].wait_recv()
            for k, l in kls:
                part[k, l, i, a, :] = part[k, l, i, a, :] + ybuf[first, k, l, a, :]
            copies[then].start()

    def y_step3(n, ks):
        copies = y_copies(n, ks)
        kls, a = blocks(n, ks)
        for o, pair in enumerate(((3, 4), (1, 5))):
            for c in pair:
                copies[c].wait_recv()
            i = base + y * 2 + o
            for k, l in kls:
                part[k, l, i, a, :] = part[k, l, i, a, :] + ybuf[pair[0], k, l, a, :] + ybuf[pair[1], k, l, a, :]
        z_copy(n, ks).start()

    def routes(k, h, op, xps=range(NX)):
        if k == 0:
            zk = z
        elif k == 1:
            zk = jnp.where(z == 1, 3, jnp.where(z == 3, 2, 1))
        else:
            zk = jnp.where(z == 0, 3, 0)
        for xp in xps:
            src = piece.at[k, xp, h]
            valid = jnp.where(gt == 1, xp <= x, xp >= x) if k == 0 else jnp.bool_(True)
            here = xp == x

            def send(device, p, n):
                c = remote(src, rall.at[p, h], rs.at[k, xp, h, n], rr.at[p, h], device)
                if op == "start":
                    c.start()
                else:
                    c.wait_send()

            def keep(p):
                if op == "start":
                    pltpu.make_async_copy(src, rall.at[p, h], rr.at[p, h]).start()

            if k == 0:
                @pl.when(valid)
                def _():
                    keep(z * 4 + xp)
            else:
                send(dev(zk, x, zl, y, core), z * 4 + xp, 1)

                @pl.when(here)
                def _():
                    keep(zk * 4 + x)

            @pl.when(jnp.logical_and(valid, jnp.logical_not(here)))
            def _():
                send(dev(z, xp, zl, y, core), zk * 4 + x, 0)

    lane = lax.broadcasted_iota(jnp.int32, (12, 128), 1)

    def pack(k, xp, h, first):
        r = [square[pl.ds(first + n, 12, stride=4), :] for n in range(4)]
        p = piece.at[k, xp, h]
        p[pl.ds(0, 12, stride=3), :] = jnp.where(lane < 96, r[0], pltpu.roll(r[1], 96, 1))
        p[pl.ds(1, 12, stride=3), :] = jnp.where(lane < 64, pltpu.roll(r[1], 96, 1), pltpu.roll(r[2], 64, 1))
        p[pl.ds(2, 12, stride=3), :] = jnp.where(lane < 32, pltpu.roll(r[2], 64, 1), pltpu.roll(r[3], 32, 1))

    def block(k, xp, a, an):
        v = [part[k, l, base + y * 2 + zl, a:a + an] + zbuf[k, l, a:a + an] for l in range(LT)]
        turn = [v[l] if l == xp else pltpu.roll(v[l], (l - xp) % 4 * 32, 1) for l in range(LT)]
        tall = lax.broadcasted_iota(jnp.int32, (an, 128), 1)
        return jnp.where(tall < 32, turn[0], jnp.where(tall < 64, turn[1], turn[2]))

    def final_half(k, h):
        for xp in range(NX):
            square[0:48] = block(k, xp, h * 48, 48)
            pack(k, xp, h, 0)
            routes(k, h, "start", (xp,))

    def final_turned(k):
        for xp in range(NX):
            w = block(k, xp, 0, VB)
            square[...] = jnp.concatenate([w, jnp.zeros((128 - VB, 128), F32)], axis=0).T
            for h in range(2):
                pack(k, xp, h, h * 48)
                routes(k, h, "start", (xp,))

    def final(k, hs):
        @pl.when(gt == 1)
        def _():
            for h in hs:
                final_half(k, h)

        if 1 in hs:
            @pl.when(gt == 0)
            def _():
                final_turned(k)

    def gather(j):
        for d in range(2):
            g_from(j, d).wait_recv()
            g_forward(j, d).start()
            if j < 2:
                g_chunk(j + 1, d).start()
        convert_g(xl, j)
        convert_g(xr, j)

    def behind(j):
        for d in range(2):
            g_behind(j, d).wait_recv()
        convert_g(x2, j)

    gather(0)
    pump(0)
    behind(0)
    stage1(0, 1)
    stage2(0, 1)
    core_copy(0, 1).start()
    pump(1)
    y_step1(0, 1)
    gather(1)
    y_step2(0, 1)
    behind(1)
    pump(2)
    stage1(1, 1)
    stage2(1, 1)
    core_copy(1, 1).start()
    y_step3(0, 1)

    def fetch(ks, m):
        for k in range(1, 1 + ks):
            if k == 1:
                p_wait(1, m)
            else:
                @pl.when(z == 2)
                def _():
                    p_wait(2, m)
            convert_s(k, m)

    def rest(ks):
        y_step1(1, 1)

        @pl.when(jnp.logical_not(ends))
        def _():
            gather(2)

        for m in range(3):
            fetch(ks, m)
        last = len(units) - 1
        for n in range(2, last + 1):
            if n == last:
                y_step1(n - 1, ks)
                y_step2(n - 2, ks)
            if units[n][0] == "rows":
                fetch(ks, units[n][1])
            stage1(n, ks)
            if 2 < n < last:
                if n == 4:
                    @pl.when(jnp.logical_not(ends))
                    def _():
                        y_step1(3, ks)
                else:
                    y_step1(n - 1, ks)
                y_step2(n - 2, ks)
            if n == 3:
                @pl.when(ends)
                def _():
                    gather(2)

                pump(3)
            stage2(n, ks)
            core_copy(n, ks).start()
            if n > 3:
                y_step3(n - 3, ks)
            if n == 3:
                @pl.when(ends)
                def _():
                    y_step1(3, ks)

                behind(2)
            if n == 4:
                pump(4)
            if n == 6:
                pump(5)
        y_step2(last - 1, ks)
        y_step1(last, ks)
        y_step3(last - 2, ks)
        for u in (2, 3, 5):
            z_copy(u, ks).wait_recv()
        for k in range(ks, 0, -1):
            final(k, (0,))
        y_step2(last, ks)
        y_step3(last - 1, ks)
        for u in (0, 1, 4):
            z_copy(u, ks).wait_recv()
        final(0, (0, 1))
        y_step3(last, ks)
        for u in (6, 7, 8):
            z_copy(u, ks).wait_recv()
        for k in range(ks, 0, -1):
            final(k, (1,))

    @pl.when(heavy)
    def _():
        rest(2)

    @pl.when(jnp.logical_not(heavy))
    def _():
        rest(1)

    for p in range(16):
        for h in range(2):
            pltpu.make_async_copy(rall.at[p, h], rall.at[p, h], rr.at[p, h]).wait()
    for s in range(out.shape[0]):
        p = partners[0, s]
        for h in range(2):
            out[s, h * 36:h * 36 + 36] = jnp.where(p >= 0, rall[jnp.maximum(p, 0), h, 0:36], 0.0)

    for j in range(LT):
        for d in range(2):
            g_chunk(j, d).wait_send()
            g_forward(j, d).wait_send()
    for n in range(5):
        t_copy(n, True).wait_send()

    @pl.when(ends)
    def _():
        for m in range(PN):
            p_relay(m).wait_send()

    def drain(n, ks):
        core_copy(n, ks).wait_send()
        for c in y_copies(n, ks):
            c.wait_send()
        z_copy(n, ks).wait_send()

    def drain_routes(k):
        for h in range(2):
            routes(k, h, "wait")

    drain_routes(0)
    drain_routes(1)

    @pl.when(heavy)
    def _():
        for n in range(len(units)):
            drain(n, 2)
        drain_routes(2)

    @pl.when(jnp.logical_not(heavy))
    def _():
        for n in range(len(units)):
            drain(n, 1)


def local(partners, cholesky, amplitudes):
    slots = partners.shape[1]
    chol = cholesky.reshape(VB, 2, CB, 2, 128).transpose(0, 1, 3, 2, 4)
    dma = pltpu.SemaphoreType.DMA
    res = pl.pallas_call(
        ladder,
        out_shape=jax.ShapeDtypeStruct((slots, 72, 128), F32),
        in_specs=[
            pl.BlockSpec(memory_space=pltpu.SMEM),
            pl.BlockSpec(memory_space=pl.ANY),
            pl.BlockSpec(memory_space=pltpu.VMEM),
        ],
        out_specs=pl.BlockSpec(memory_space=pltpu.VMEM),
        scratch_shapes=[
            pltpu.VMEM((NX, VB, 2, CB, 128), F32),
            pltpu.VMEM((3, VB, 2, CB, 128), F32),
            pltpu.VMEM((8, 128), F32),
            pltpu.VMEM((2, 4, 2, 8, 128), F32),
            pltpu.VMEM((256, 512), BF16),
            pltpu.VMEM((ROWS, 3 * QL), BF16),
            pltpu.VMEM((PN, 2 * PC * CB, 3 * QL), BF16),
            pltpu.VMEM((LT, CB * 128, 3 * QL), BF16),
            pltpu.VMEM((2, CB, ROWS, 128), BF16),
            pltpu.VMEM((3, LT, IJ, VB, 128), F32),
            pltpu.VMEM((3, LT, 8, VB, 128), F32),
            pltpu.VMEM((6, 3, LT, VB, 128), F32),
            pltpu.VMEM((3, LT, VB, 128), F32),
            pltpu.VMEM((128, 128), F32),
            pltpu.VMEM((3, NX, 2, 40, 128), F32),
            pltpu.VMEM((16, 2, 40, 128), F32),
            dma((2,)),
            dma((3, 4)), dma((3, 4)),
            dma((3, PN)), dma((3, PN)),
            dma((5,)), dma((5,)),
            dma((9,)), dma((9,)),
            dma((9, 6)), dma((9, 6)),
            dma((9,)), dma((9,)),
            dma((3, NX, 2, 2)), dma((16, 2)),
        ],
        compiler_params=pltpu.CompilerParams(
            collective_id=0, has_side_effects=True, vmem_limit_bytes=56 * 1024 * 1024
        ),
    )(partners, chol, amplitudes)
    return res.reshape(slots, 1, VB * VB)


def solution(mesh):
    return jax.shard_map(
        local,
        mesh=mesh,
        in_specs=(P("ab", None), P("ab", None, "ij"), P("ij", None)),
        out_specs=P("ab", "ij", None),
        check_vma=False,
    )
```

```python
import jax
import jax.numpy as jnp
from jax import lax
from jax.experimental import pallas as pl
from jax.experimental.pallas import tpu as pltpu
from jax.sharding import PartitionSpec as P

MESH = pl.DeviceIdType.MESH
F32 = jnp.float32
BF16 = jnp.bfloat16
VB = 96
CB = 8
QL = 256
ROWS = VB * CB
NX = 4
LT = 3
CH = 32
PC = 16
PN = 6
IJ = 16


def split(v):
    hi = v.astype(BF16)
    lo = (v - hi.astype(F32)).astype(BF16)
    return hi, lo


def ladder(
    partners, chol, amp, out,
    gbuf, sbuf, abuf, tbuf, wide, left, leftp, right, tile, part, cbuf, ybuf, zbuf, square, piece, rall,
    lsem, gs, gr, ps, pr, ts, tr, cs, cr, ys, yr, zs, zr, rs, rr,
):
    ab = lax.axis_index("ab")
    ij = lax.axis_index("ij")
    z, x = lax.div(ab, 4), lax.rem(ab, 4)
    zl, y, core = lax.div(ij, 8), lax.rem(lax.div(ij, 2), 4), lax.rem(ij, 2)

    def dev(z_, x_, zl_, y_, core_):
        return (z_ * 4 + x_, zl_ * 8 + y_ * 2 + core_)

    def mod4(v):
        return lax.rem(v + 8, 4)

    gt = jnp.where(z < 2, 1, 0)
    xl, xr, x2 = mod4(x - 1), mod4(x + 1), mod4(x + 2)
    yl, yr_, y2 = mod4(y - 1), mod4(y + 1), mod4(y + 2)
    heavy = lax.rem(z, 2) == 0
    ends = jnp.logical_or(z == 0, z == 3)

    barrier = pltpu.get_barrier_semaphore()
    peers = [dev(z, x, zl, y, 1 - core), dev(z, x, 1 - zl, y, core)]
    for n in range(1, 4):
        peers.append(dev(z, x, zl, mod4(y + n), core))
        peers.append(dev(z, mod4(x + n), zl, y, core))
        peers.append(dev(mod4(z + n), x, zl, y, core))
    for peer in peers:
        pl.semaphore_signal(barrier, inc=1, device_id=peer, device_id_type=MESH)
    own_g = chol.at[:, gt]
    local_g = pltpu.make_async_copy(own_g, gbuf.at[x], lsem.at[0])
    local_s = pltpu.make_async_copy(chol.at[:, 1 - gt], sbuf.at[0], lsem.at[1])
    local_g.start()
    local_s.start()
    row = jnp.concatenate([amp[...], jnp.zeros((1, 64), F32)], axis=1)
    abuf[...] = jnp.broadcast_to(row, (8, 128))
    pl.semaphore_wait(barrier, len(peers))

    def remote(src, dst, send, recv, device):
        return pltpu.make_async_remote_copy(
            src_ref=src, dst_ref=dst, send_sem=send, recv_sem=recv, device_id=device, device_id_type=MESH
        )

    to_right, to_left = dev(z, xr, zl, y, core), dev(z, xl, zl, y, core)

    def g_chunk(j, d):
        return remote(
            chol.at[pl.ds(j * CH, CH), gt], gbuf.at[x, pl.ds(j * CH, CH)], gs.at[j, d], gr.at[j, d],
            (to_right, to_left)[d],
        )

    def g_from(j, d):
        at = gbuf.at[(xl, xr)[d], pl.ds(j * CH, CH)]
        return remote(at, at, gs.at[j, d], gr.at[j, d], (to_right, to_left)[d])

    def g_forward(j, d):
        at = gbuf.at[(xl, xr)[d], pl.ds(j * CH + d * 16, 16)]
        return remote(at, at, gs.at[j, 2 + d], gr.at[j, 2 + d], (to_right, to_left)[d])

    def g_behind(j, d):
        at = gbuf.at[x2, pl.ds(j * CH + d * 16, 16)]
        return remote(at, at, gs.at[j, 2 + d], gr.at[j, 2 + d], (to_right, to_left)[d])

    def p_send(m):
        rows = pl.ds(m * PC, PC)
        to = jnp.where(ends, 2, 1)
        return remote(
            chol.at[rows, 1 - lax.rem(z, 2)], sbuf.at[to, rows], ps.at[0, m], pr.at[to, m],
            dev(3 * (1 - lax.rem(z, 2)), x, zl, y, core),
        )

    def p_send_up(m):
        rows = pl.ds(m * PC, PC)
        return remote(
            chol.at[rows, 1], sbuf.at[1, rows], ps.at[1, m], pr.at[1, m], dev(2, x, zl, y, core)
        )

    def p_relay(m):
        rows = pl.ds(m * PC, PC)
        to = jnp.where(z == 0, 1, 2)
        return remote(
            sbuf.at[2, rows], sbuf.at[to, rows], ps.at[2, m], pr.at[to, m], dev(to, x, zl, y, core)
        )

    def p_wait(k, m):
        at = sbuf.at[k, pl.ds(m * PC, PC)]
        remote(at, at, ps.at[0, m], pr.at[k, m], to_right).wait_recv()

    for d in range(2):
        g_chunk(0, d).start()
    def p_start(m):
        p_send(m).start()

        @pl.when(z == 1)
        def _():
            p_send_up(m).start()

    def pump(m):
        p_send(m).wait_send()

        @pl.when(z == 1)
        def _():
            p_send_up(m).wait_send()

        if m + 2 < PN:
            p_start(m + 2)

        @pl.when(ends)
        def _():
            p_wait(2, m)
            p_relay(m).start()

    p_start(0)
    p_start(1)
    def t_copy(n, send):
        if n == 0:
            at, device = tbuf.at[core if send else 1 - core, y, zl], dev(z, x, zl, y, 1 - core)
        elif n == 1:
            at, device = tbuf.at[:, y, zl if send else 1 - zl], dev(z, x, 1 - zl, y, core)
        else:
            at, device = tbuf.at[:, y if send else mod4(y - n + 1)], dev(z, x, zl, mod4(y + n - 1), core)
        return remote(at, at, ts.at[n], tr.at[n], device)

    tbuf[core, y, zl] = abuf[...]
    t_copy(0, True).start()

    gview = gbuf.reshape(NX, VB * 2 * CB, 128)

    def convert_g(n, j):
        for e in range(CB):
            v = jnp.concatenate(
                [gview[n, pl.ds(j * CH * 16 + h * CB + e, CH, stride=2 * CB), :] for h in range(2)], axis=1
            )
            hi, lo = split(v)
            at = pl.ds(pl.multiple_of(e * 128 + n * CH, CH), CH)
            right[j, at, 0:QL] = hi
            right[j, at, QL:2 * QL] = lo
            right[j, at, 2 * QL:3 * QL] = hi

    def convert_s(k, m):
        for h in range(2):
            v = sbuf[k, pl.ds(m * PC, PC), h].reshape(PC * CB, 128)
            hi, lo = split(v)
            to = left.at[pl.ds(m * PC * CB, PC * CB)] if k == 0 else leftp.at[m, pl.ds((k - 1) * PC * CB, PC * CB)]
            to[:, h * 128:h * 128 + 128] = hi
            to[:, QL + h * 128:QL + h * 128 + 128] = hi
            to[:, 2 * QL + h * 128:2 * QL + h * 128 + 128] = lo

    local_g.wait()
    local_s.wait()
    for j in range(LT):
        convert_g(x, j)
    for m in range(PN):
        convert_s(0, m)

    for n in range(2):
        t_copy(n, False).wait_recv()
        for o in ((1,), (2, 3, 4))[n]:
            t_copy(o, True).start()
    for n in range(2, 5):
        t_copy(n, False).wait_recv()
    source = lax.broadcasted_iota(jnp.int32, (128, 512), 0)
    target = lax.broadcasted_iota(jnp.int32, (128, 512), 1)
    outer, inner = lax.div(target, 64), lax.rem(target, 8)
    pick = jnp.where(source == jnp.where(gt == 1, inner * 8 + outer, outer * 8 + inner), 1.0, 0.0).astype(BF16)
    same = lax.rem(source, 8) == lax.rem(lax.div(target, 8), 8)
    for n, v in enumerate(split(tbuf.reshape(IJ, 8, 128)[:, 0, :])):
        w = jnp.dot(v, pick, preferred_element_type=F32)
        w = jnp.broadcast_to(w[:, None, :], (IJ, 8, 512)).reshape(128, 512)
        wide[n * 128:(n + 1) * 128] = jnp.where(same, w, 0.0).astype(BF16)

    units = [("own", 0), ("own", 1), ("half", 0), ("half", 1), ("own", 2), ("half", 2)]
    units += [("rows", m) for m in range(3, PN)]

    def stage1(n, ks):
        kind, v = units[n]
        size = 256 if kind == "own" else 128 * ks

        def column(en, carry):
            at = pl.ds(en * 256, 256) if isinstance(en, int) else pl.ds(pl.multiple_of(en * 256, 256), 256)
            for r in range(3):
                if kind == "own":
                    lhs = left[r * 256:(r + 1) * 256, :]
                else:
                    lhs = leftp[r if kind == "half" else v, 0:size, :]
                t = lax.dot_general(
                    lhs, right[r if kind == "rows" else v, at, :],
                    (((1,), (1,)), ((), ())), preferred_element_type=F32,
                )
                hi, lo = split(t)
                for u in range(256 // 128):
                    tile[0, en * 2 + u, r * size:(r + 1) * size, :] = hi[:, u * 128:(u + 1) * 128]
                    tile[1, en * 2 + u, r * size:(r + 1) * size, :] = lo[:, u * 128:(u + 1) * 128]
            return carry

        for en in range(CB * 128 // 256):
            column(en, 0)

    def stage2(n, ks):
        kind, w = units[n]

        many = 4 if kind == "own" else 2 * ks

        def rows(it, carry):
            cols = []
            for h in range(2):
                at = [(it * many + u) * 64 for u in range(many)]
                cols.append(
                    jnp.concatenate(
                        [jnp.concatenate([tile[h, e, pl.ds(b, 64), :] for e in range(CB)], axis=0) for b in at], axis=1
                    )
                )
            r = jnp.dot(wide[...], cols[0], preferred_element_type=F32)
            q = jnp.dot(wide[0:128], cols[1], preferred_element_type=F32)
            r = r[:128] + r[128:] + q
            for u in range(many):
                v = r[:, u * 128:(u + 1) * 128].reshape(IJ, 8, 128)
                if kind == "own":
                    part[0, w, :, pl.ds((it * many + u) * 8, 8), :] = v
                elif kind == "half":
                    part[1 + u // 2, w, :, pl.ds(it * PC + u % 2 * 8, 8), :] = v
                else:
                    part[1 + u // 2, it, :, pl.ds(w * PC + u % 2 * 8, 8), :] = v
            return carry

        for it in range(3):
            rows(it, 0)

    base, away = core * 8, (1 - core) * 8
    sibling = dev(z, x, zl, y, 1 - core)
    y_left, y_right = dev(z, x, zl, yl, core), dev(z, x, zl, yr_, core)
    z_other = dev(z, x, 1 - zl, y, core)

    def reach(n):
        kind, v = units[n]
        return {"own": (v, 1, 0, VB), "half": (v, 1, 0, 3 * PC), "rows": (0, LT, v * PC, PC)}[kind]

    def spans(n, ks):
        l, ln, a, an = reach(n)
        return pl.ds(0, 1) if units[n][0] == "own" else pl.ds(1, ks), pl.ds(l, ln), pl.ds(a, an)

    def blocks(n, ks):
        l, ln, a, an = reach(n)
        ks_ = [0] if units[n][0] == "own" else range(1, 1 + ks)
        return [(k, l_) for k in ks_ for l_ in range(l, l + ln)], slice(a, a + an)

    def core_copy(n, ks):
        k, l, a = spans(n, ks)
        return remote(
            part.at[k, l, pl.ds(away, 8), a], cbuf.at[k, l, pl.ds(0, 8), a], cs.at[n], cr.at[n], sibling
        )

    def y_copies(n, ks):
        k, l, a = spans(n, ks)

        def one(c, y_, o, device):
            return remote(
                part.at[k, l, base + y_ * 2 + o, a], ybuf.at[c, k, l, a], ys.at[n, c], yr.at[n, c], device
            )

        return [
            one(0, y2, 0, y_right), one(1, yr_, 1, y_right), one(2, y2, 1, y_left),
            one(3, yl, 0, y_left), one(4, yr_, 0, y_right), one(5, yl, 1, y_left),
        ]

    def z_copy(n, ks):
        k, l, a = spans(n, ks)
        return remote(
            part.at[k, l, base + y * 2 + (1 - zl), a], zbuf.at[k, l, a], zs.at[n], zr.at[n], z_other
        )

    def y_step1(n, ks):
        core_copy(n, ks).wait_recv()
        kls, a = blocks(n, ks)

        def add(i, carry):
            for k, l in kls:
                part[k, l, base + i, a, :] = part[k, l, base + i, a, :] + cbuf[k, l, i, a, :]
            return carry

        lax.fori_loop(0, 8, add, 0)
        for c in y_copies(n, ks)[:4]:
            c.start()

    def y_step2(n, ks):
        copies = y_copies(n, ks)
        kls, a = blocks(n, ks)
        for first, i, then in ((0, base + yr_ * 2, 4), (2, base + yl * 2 + 1, 5)):
            copies[first].wait_recv()
            for k, l in kls:
                part[k, l, i, a, :] = part[k, l, i, a, :] + ybuf[first, k, l, a, :]
            copies[then].start()

    def y_step3(n, ks):
        copies = y_copies(n, ks)
        kls, a = blocks(n, ks)
        for o, pair in enumerate(((3, 4), (1, 5))):
            for c in pair:
                copies[c].wait_recv()
            i = base + y * 2 + o
            for k, l in kls:
                part[k, l, i, a, :] = part[k, l, i, a, :] + ybuf[pair[0], k, l, a, :] + ybuf[pair[1], k, l, a, :]
        z_copy(n, ks).start()

    def routes(k, h, op, xps=range(NX)):
        if k == 0:
            zk = z
        elif k == 1:
            zk = jnp.where(z == 1, 3, jnp.where(z == 3, 2, 1))
        else:
            zk = jnp.where(z == 0, 3, 0)
        for xp in xps:
            src = piece.at[k, xp, h]
            valid = jnp.where(gt == 1, xp <= x, xp >= x) if k == 0 else jnp.bool_(True)
            here = xp == x

            def send(device, p, n):
                c = remote(src, rall.at[p, h], rs.at[k, xp, h, n], rr.at[p, h], device)
                if op == "start":
                    c.start()
                else:
                    c.wait_send()

            def keep(p):
                if op == "start":
                    pltpu.make_async_copy(src, rall.at[p, h], rr.at[p, h]).start()

            if k == 0:
                @pl.when(valid)
                def _():
                    keep(z * 4 + xp)
            else:
                send(dev(zk, x, zl, y, core), z * 4 + xp, 1)

                @pl.when(here)
                def _():
                    keep(zk * 4 + x)

            @pl.when(jnp.logical_and(valid, jnp.logical_not(here)))
            def _():
                send(dev(z, xp, zl, y, core), zk * 4 + x, 0)

    lane = lax.broadcasted_iota(jnp.int32, (12, 128), 1)

    def pack(k, xp, h, first):
        r = [square[pl.ds(first + n, 12, stride=4), :] for n in range(4)]
        p = piece.at[k, xp, h]
        p[pl.ds(0, 12, stride=3), :] = jnp.where(lane < 96, r[0], pltpu.roll(r[1], 96, 1))
        p[pl.ds(1, 12, stride=3), :] = jnp.where(lane < 64, pltpu.roll(r[1], 96, 1), pltpu.roll(r[2], 64, 1))
        p[pl.ds(2, 12, stride=3), :] = jnp.where(lane < 32, pltpu.roll(r[2], 64, 1), pltpu.roll(r[3], 32, 1))

    def block(k, xp, a, an):
        v = [part[k, l, base + y * 2 + zl, a:a + an] + zbuf[k, l, a:a + an] for l in range(LT)]
        turn = [v[l] if l == xp else pltpu.roll(v[l], (l - xp) % 4 * 32, 1) for l in range(LT)]
        tall = lax.broadcasted_iota(jnp.int32, (an, 128), 1)
        return jnp.where(tall < 32, turn[0], jnp.where(tall < 64, turn[1], turn[2]))

    def final_half(k, h):
        for xp in range(NX):
            square[0:48] = block(k, xp, h * 48, 48)
            pack(k, xp, h, 0)
            routes(k, h, "start", (xp,))

    def final_turned(k):
        for xp in range(NX):
            w = block(k, xp, 0, VB)
            square[...] = jnp.concatenate([w, jnp.zeros((128 - VB, 128), F32)], axis=0).T
            for h in range(2):
                pack(k, xp, h, h * 48)
                routes(k, h, "start", (xp,))

    def final(k, hs):
        @pl.when(gt == 1)
        def _():
            for h in hs:
                final_half(k, h)

        if 1 in hs:
            @pl.when(gt == 0)
            def _():
                final_turned(k)

    def gather(j):
        for d in range(2):
            g_from(j, d).wait_recv()
            g_forward(j, d).start()
            if j < 2:
                g_chunk(j + 1, d).start()
        convert_g(xl, j)
        convert_g(xr, j)

    def behind(j):
        for d in range(2):
            g_behind(j, d).wait_recv()
        convert_g(x2, j)

    gather(0)
    pump(0)
    behind(0)
    stage1(0, 1)
    stage2(0, 1)
    core_copy(0, 1).start()
    pump(1)
    y_step1(0, 1)
    gather(1)
    y_step2(0, 1)
    behind(1)
    pump(2)
    stage1(1, 1)
    stage2(1, 1)
    core_copy(1, 1).start()
    y_step3(0, 1)

    def fetch(ks, m):
        for k in range(1, 1 + ks):
            if k == 1:
                p_wait(1, m)
            else:
                @pl.when(z == 2)
                def _():
                    p_wait(2, m)
            convert_s(k, m)

    def rest(ks):
        y_step1(1, 1)

        @pl.when(jnp.logical_not(ends))
        def _():
            gather(2)

        for m in range(3):
            fetch(ks, m)
        last = len(units) - 1
        for n in range(2, last + 1):
            if n >= 6:
                y_step1(n - 1, ks)
            if n == last:
                y_step2(n - 2, ks)
            if units[n][0] == "rows":
                fetch(ks, units[n][1])
            stage1(n, ks)
            if 2 < n < last:
                if n == 4:
                    @pl.when(jnp.logical_not(ends))
                    def _():
                        y_step1(3, ks)
                elif n < 6:
                    y_step1(n - 1, ks)
                y_step2(n - 2, ks)
            if n == 3:
                @pl.when(ends)
                def _():
                    gather(2)

                pump(3)
            stage2(n, ks)
            core_copy(n, ks).start()
            if n > 3:
                y_step3(n - 3, ks)
            if n == 3:
                @pl.when(ends)
                def _():
                    y_step1(3, ks)

                behind(2)
            if n == 4:
                pump(4)
            if n == 6:
                pump(5)
        y_step2(last - 1, ks)
        y_step1(last, ks)
        y_step3(last - 2, ks)
        for u in (2, 3, 5):
            z_copy(u, ks).wait_recv()
        for k in range(ks, 0, -1):
            final(k, (0,))
        y_step2(last, ks)
        y_step3(last - 1, ks)
        for u in (0, 1, 4):
            z_copy(u, ks).wait_recv()
        final(0, (0, 1))
        y_step3(last, ks)
        for u in (6, 7, 8):
            z_copy(u, ks).wait_recv()
        for k in range(ks, 0, -1):
            final(k, (1,))

    @pl.when(heavy)
    def _():
        rest(2)

    @pl.when(jnp.logical_not(heavy))
    def _():
        rest(1)

    for p in range(16):
        for h in range(2):
            pltpu.make_async_copy(rall.at[p, h], rall.at[p, h], rr.at[p, h]).wait()
    for s in range(out.shape[0]):
        p = partners[0, s]
        for h in range(2):
            out[s, h * 36:h * 36 + 36] = jnp.where(p >= 0, rall[jnp.maximum(p, 0), h, 0:36], 0.0)

    for j in range(LT):
        for d in range(2):
            g_chunk(j, d).wait_send()
            g_forward(j, d).wait_send()
    for n in range(5):
        t_copy(n, True).wait_send()

    @pl.when(ends)
    def _():
        for m in range(PN):
            p_relay(m).wait_send()

    def drain(n, ks):
        core_copy(n, ks).wait_send()
        for c in y_copies(n, ks):
            c.wait_send()
        z_copy(n, ks).wait_send()

    def drain_routes(k):
        for h in range(2):
            routes(k, h, "wait")

    drain_routes(0)
    drain_routes(1)

    @pl.when(heavy)
    def _():
        for n in range(len(units)):
            drain(n, 2)
        drain_routes(2)

    @pl.when(jnp.logical_not(heavy))
    def _():
        for n in range(len(units)):
            drain(n, 1)


def local(partners, cholesky, amplitudes):
    slots = partners.shape[1]
    chol = cholesky.reshape(VB, 2, CB, 2, 128).transpose(0, 1, 3, 2, 4)
    dma = pltpu.SemaphoreType.DMA
    res = pl.pallas_call(
        ladder,
        out_shape=jax.ShapeDtypeStruct((slots, 72, 128), F32),
        in_specs=[
            pl.BlockSpec(memory_space=pltpu.SMEM),
            pl.BlockSpec(memory_space=pl.ANY),
            pl.BlockSpec(memory_space=pltpu.VMEM),
        ],
        out_specs=pl.BlockSpec(memory_space=pltpu.VMEM),
        scratch_shapes=[
            pltpu.VMEM((NX, VB, 2, CB, 128), F32),
            pltpu.VMEM((3, VB, 2, CB, 128), F32),
            pltpu.VMEM((8, 128), F32),
            pltpu.VMEM((2, 4, 2, 8, 128), F32),
            pltpu.VMEM((256, 512), BF16),
            pltpu.VMEM((ROWS, 3 * QL), BF16),
            pltpu.VMEM((PN, 2 * PC * CB, 3 * QL), BF16),
            pltpu.VMEM((LT, CB * 128, 3 * QL), BF16),
            pltpu.VMEM((2, CB, ROWS, 128), BF16),
            pltpu.VMEM((3, LT, IJ, VB, 128), F32),
            pltpu.VMEM((3, LT, 8, VB, 128), F32),
            pltpu.VMEM((6, 3, LT, VB, 128), F32),
            pltpu.VMEM((3, LT, VB, 128), F32),
            pltpu.VMEM((128, 128), F32),
            pltpu.VMEM((3, NX, 2, 40, 128), F32),
            pltpu.VMEM((16, 2, 40, 128), F32),
            dma((2,)),
            dma((3, 4)), dma((3, 4)),
            dma((3, PN)), dma((3, PN)),
            dma((5,)), dma((5,)),
            dma((9,)), dma((9,)),
            dma((9, 6)), dma((9, 6)),
            dma((9,)), dma((9,)),
            dma((3, NX, 2, 2)), dma((16, 2)),
        ],
        compiler_params=pltpu.CompilerParams(
            collective_id=0, has_side_effects=True, vmem_limit_bytes=56 * 1024 * 1024
        ),
    )(partners, chol, amplitudes)
    return res.reshape(slots, 1, VB * VB)


def solution(mesh):
    return jax.shard_map(
        local,
        mesh=mesh,
        in_specs=(P("ab", None), P("ab", None, "ij"), P("ij", None)),
        out_specs=P("ab", "ij", None),
        check_vma=False,
    )
```
